32 devices in a mesh: seq: 16 (over z, x, core), head: 2 (over y).
Axes of the slice: x: 2, y: 2, z: 4, core: 2. Of those that a mesh axis runs over, the one named last changes fastest.
Arguments:
- queries: bfloat16 [6144, 4096], P('seq', 'head'), may hold values from -8 to 8
- keys: bfloat16 [6144, 4096], P('seq', 'head'), may hold values from -8 to 8
- values: bfloat16 [6144, 4096], P('seq', 'head'), may hold values from -6 to 6
- target_row: int32 [6144], P('seq'), may hold values from 0 to 6143, as said below
- doc_lengths: int32 [32], replicated, may hold values from 0 to 3072, as said below
Outputs:
- mixed: bfloat16 [6144, 4096], P('seq', 'head')
The draws below stay inside these ranges and needn't reach their ends.
Inputs may be any that keep to these rules, and one draw needn't show every extreme that they name: `target_row`: A permutation of the rows. The rows of one device go to at most 36 rows of any one device's block of 384 rows in document order, and every device sends exactly 36 rows to some device. `doc_lengths`: they sum to 6144; zero lengths occur; no document crosses a multiple of 3072 rows, and some document fills the rows between two such multiples.
All inputs are finite; a program needn't handle non-finite values.
Results may differ from the reference program's by a relative error of at most 0.0035.
Values may be sent and summed in bfloat16 or wider, within the bound.
No kernel may reach another device: no remote copies, remote signals or barrier semaphores. Data moves between devices by JAX's collectives and lax.ppermute only.
A program may use at most 64 MiB of HBM per device.

```python
import math
import jax
import jax.numpy as jnp
from jax import lax

HEADS = 32
HD = 128
ROWS_DEV = 384
GROUP = 16
TOKENS = 6144


def draw_queries(key, part):
    key = jax.random.fold_in(key, 31)
    first_key = jax.random.fold_in(key, 0)
    noise = jax.random.normal(first_key, (TOKENS, HEADS * HD), jnp.float32)
    return jnp.clip(noise, -6.0, 6.0).astype(jnp.bfloat16)


def draw_keys(key, part):
    key = jax.random.fold_in(key, 37)
    noise = jax.random.normal(key, (TOKENS, HEADS * HD), jnp.float32)
    return jnp.clip(noise, -6.0, 6.0).astype(jnp.bfloat16)


def draw_target_row(key, part):
    key = jax.random.fold_in(key, 11)
    count = TOKENS // ROWS_DEV
    rows = ROWS_DEV
    base_count = rows // count
    extra = base_count // 2
    first_key, second_key, third_key = jax.random.split(key, 3)
    sigma = jax.random.permutation(first_key, count).astype(jnp.int32)
    tau = jnp.roll(sigma, -1)
    devices = jnp.arange(count, dtype=jnp.int32)
    counts = base_count + extra * ((devices[None, :] == sigma[:, None]).astype(jnp.int32) - (devices[None, :] == tau[:, None]).astype(jnp.int32))
    row_cum = jnp.cumsum(counts, axis=1)
    positions = jnp.arange(rows, dtype=jnp.int32)
    target_device = jnp.sum((row_cum[:, None, :] <= positions[None, :, None]).astype(jnp.int32), axis=2)
    row_start = row_cum - counts
    within = positions[None, :] - jnp.take_along_axis(row_start, target_device, axis=1)
    col_start = jnp.cumsum(counts, axis=0) - counts
    rank = jnp.take_along_axis(col_start, target_device, axis=1) + within
    perm_target = jax.vmap(lambda each: jax.random.permutation(each, rows))(jax.random.split(second_key, count)).astype(jnp.int32)
    perm_loader = jax.vmap(lambda each: jax.random.permutation(each, rows))(jax.random.split(third_key, count)).astype(jnp.int32)
    target_place = target_device * rows + perm_target[target_device, rank]
    loader_place = devices[:, None] * rows + perm_loader
    result = jnp.zeros((count * rows,), jnp.int32).at[loader_place.reshape(-1)].set(target_place.reshape(-1))
    return result


def draw_doc_lengths(key, part):
    key = jax.random.fold_in(key, 23)
    count = TOKENS // ROWS_DEV
    rows = ROWS_DEV
    half = rows // 2
    half_group = GROUP // 2
    keys_list = jax.random.split(key, 5)
    devices = jnp.arange(count, dtype=jnp.int32)
    first = devices * rows + jax.random.randint(keys_list[0], (count,), 0, half, jnp.int32)
    second = devices * rows + half + jax.random.randint(keys_list[1], (count,), 0, half, jnp.int32)
    on_first = jax.random.randint(keys_list[2], (count,), 0, 2, jnp.int32)
    on_second = jax.random.randint(keys_list[3], (count,), 0, 2, jnp.int32)
    full_half = jax.random.randint(keys_list[4], (), 0, 2 * (count // GROUP), jnp.int32)
    starting = devices % half_group == 0
    first = jnp.where(starting, devices * rows, first)
    keep_first = jnp.where(starting, 1, on_first)
    candidates = jnp.stack([first, second], axis=1).reshape(-1)
    keeping = jnp.stack([keep_first, on_second], axis=1).reshape(-1)
    entries = jnp.arange(2 * count, dtype=jnp.int32)
    entry_half = entries // (2 * half_group)
    in_full = entry_half == full_half
    half_start = entry_half * (half_group * rows)
    candidates = jnp.where(in_full, half_start, candidates)
    keeping = jnp.where(in_full, (entries % (2 * half_group) == 0).astype(jnp.int32), keeping)
    bounds = lax.cummax(jnp.where(keeping == 1, candidates, 0), axis=0)
    ends = jnp.concatenate([bounds[1:], jnp.full((1,), count * rows, jnp.int32)])
    return (ends - bounds).astype(jnp.int32)


def level_of(own_key, extent, cuts, smallest, top_value):
    factor_of = 1.0
    for position, blocks in cuts:
        steps = jax.random.uniform(jax.random.fold_in(jax.random.fold_in(own_key, 6), position), (blocks,), jnp.float32, smallest / len(cuts), top_value / len(cuts))
        factor_of = factor_of * jnp.repeat(jnp.exp(steps), extent[position] // blocks).reshape((-1,) + (1,) * (len(extent) - 1 - position))
    return factor_of


def bell_draw(own_key, shape, scale, limit, cuts=(), kind=jnp.bfloat16):
    values = jax.random.normal(own_key, shape, jnp.float32) * scale
    if len(cuts) > 0:
        values = level_of(own_key, shape, cuts, -0.22, 0.18) * values
    return jnp.clip(values, min=-limit, max=limit).astype(kind)


def setup_inputs(seed: int = 0) -> dict:
    streams_of = jax.random.split(jax.random.key(seed), 6)
    queries = draw_queries(jax.random.fold_in(streams_of[5], 71), 0)
    keys = draw_keys(jax.random.fold_in(streams_of[5], 71), 0)
    values = bell_draw(streams_of[2], (TOKENS, HEADS * HD), 1.0, 6.0, ((0, 16), (1, 2)))
    target_row = draw_target_row(jax.random.fold_in(streams_of[5], 71), 0)
    doc_lengths = draw_doc_lengths(jax.random.fold_in(streams_of[5], 71), 0)
    return dict(queries=queries, keys=keys, values=values, target_row=target_row, doc_lengths=doc_lengths)


def reference(queries, keys, values, target_row, doc_lengths):
    width = HEADS * HD
    span = GROUP * ROWS_DEV
    groups = TOKENS // span
    scale = 1.0 / math.sqrt(HD)

    def place(source):
        return jnp.zeros((TOKENS, width), source.dtype).at[target_row].set(source)
    q_rows = place(queries)
    k_rows = place(keys)
    v_rows = place(values)
    starts = jnp.cumsum(doc_lengths) - doc_lengths

    def one_group(index):
        first = index * span
        query_group = lax.dynamic_slice_in_dim(q_rows, first, span, 0).reshape(span, HEADS, HD)
        key_group = lax.dynamic_slice_in_dim(k_rows, first, span, 0).reshape(span, HEADS, HD)
        value_group = lax.dynamic_slice_in_dim(v_rows, first, span, 0).reshape(span, HEADS, HD)
        positions = first + jnp.arange(span, dtype=jnp.int32)
        labels = lax.optimization_barrier(jnp.sum((starts[None, :] <= positions[:, None]).astype(jnp.int32), axis=1))

        def one_head(head):
            query_head = lax.dynamic_index_in_dim(query_group, head, 1, keepdims=False)
            key_head = lax.dynamic_index_in_dim(key_group, head, 1, keepdims=False)
            value_head = lax.dynamic_index_in_dim(value_group, head, 1, keepdims=False)
            pieces = []
            for block in range(span // 512):
                lower = block * 512
                upper = lower + 512
                scores = jnp.dot(query_head[lower:upper], key_head[:upper].T, preferred_element_type=jnp.float32) * scale
                allowed = (labels[lower:upper, None] == labels[None, :upper]) & (positions[None, :upper] <= positions[lower:upper, None])
                scores = jnp.where(allowed, scores, -1e+30)
                top = lax.optimization_barrier(jnp.max(scores, axis=1, keepdims=True))
                weights = jnp.where(allowed, jnp.exp(scores - top), 0.0)
                total = lax.optimization_barrier(jnp.sum(weights, axis=1, keepdims=True))
                mixed = jnp.dot(weights.astype(jnp.bfloat16), value_head[:upper], preferred_element_type=jnp.float32) / total
                pieces.append(mixed.astype(jnp.bfloat16))
            return jnp.concatenate(pieces, axis=0)
        heads_out = lax.map(one_head, jnp.arange(HEADS, dtype=jnp.int32))
        return jnp.transpose(heads_out, (1, 0, 2)).reshape(span, width)
    result = lax.map(one_group, jnp.arange(groups, dtype=jnp.int32))
    return result.reshape(TOKENS, width)
```

```python
import functools
import math

import jax
import jax.numpy as jnp
from jax import lax
from jax.experimental import pallas as pl
from jax.experimental.pallas import tpu as pltpu
from jax.sharding import PartitionSpec as P

HD = 128
SUB = 16
BASE = 64
NEG = -1e30
EXP2_SCALE = math.log2(math.e) / math.sqrt(HD)
VMEM_LIMIT = 40 * 1024 * 1024


def rounded_up(count, multiple):
    return -(-count // multiple) * multiple


def sort_kernel(units, span_rows, cap, total, target_col_ref, target_row_ref, q_ref, k_ref, v_ref, out_ref, onehot, notes):
    rows = q_ref.shape[0]
    lanes = 3 * HD

    @pl.when(pl.program_id(0) == 0)
    def _():
        across = target_row_ref[...]
        down = target_col_ref[...]
        unit = jnp.zeros_like(across)
        for u in range(1, units):
            unit += (across >= u * span_rows).astype(jnp.int32)
        inner = across - unit * span_rows
        before = (down < across) & (down >= unit * span_rows)
        place = jnp.sum(before.astype(jnp.int32), axis=0, keepdims=True)
        slot = jnp.where(place < cap, unit * total + place, -1)
        slots = lax.broadcasted_iota(jnp.int32, (units * total, rows), 0)
        onehot[...] = jnp.where(slots == slot, 1.0, 0.0).astype(jnp.bfloat16)
        crowded = jnp.max(jnp.where(place >= cap, 1.0, 0.0), axis=1, keepdims=True)
        high = inner // BASE
        kind = lax.broadcasted_iota(jnp.int32, (SUB, rows), 0)
        digits = jnp.where(kind == 0, high + 1, jnp.where(kind == 1, inner - high * BASE, 0))
        digits = digits.astype(jnp.float32).astype(jnp.bfloat16)
        spread = lax.broadcasted_iota(jnp.int32, (lanes, rows), 0)
        line = lax.broadcasted_iota(jnp.int32, (total, lanes), 0)
        for u in range(units):
            mine = jnp.where((spread == place) & (unit == u), 1.0, 0.0).astype(jnp.bfloat16)
            along = lax.dot_general(
                digits, mine, (((1,), (1,)), ((), ())), preferred_element_type=jnp.float32
            )
            note = jnp.where(line == total - 3, along[0:1], jnp.where(line == total - 2, along[1:2], 0.0))
            note = jnp.where(line == total - 1, crowded, note)
            notes[u * total : (u + 1) * total, :] = note.astype(jnp.bfloat16)

    for m in range(q_ref.shape[1] // HD):
        cols = slice(m * HD, (m + 1) * HD)
        block = jnp.concatenate([q_ref[:, cols], k_ref[:, cols], v_ref[:, cols]], axis=1)
        sent = jnp.dot(onehot[...], block, preferred_element_type=jnp.float32).astype(jnp.bfloat16)
        out_ref[:, m] = (sent + notes[...]).reshape(units, total, lanes)


def sort_rows(queries, keys, values, target_row, units, span, cap, total, chunk):
    rows = queries.shape[0]
    steps = math.gcd(span, 2)
    count = span // steps
    column = pl.BlockSpec((rows, count * HD), lambda n: (0, chunk * steps + n))
    sent = pl.pallas_call(
        functools.partial(sort_kernel, units, span * rows, cap, total),
        grid=(steps,),
        out_shape=jax.ShapeDtypeStruct((units, span, total, 3 * HD), jnp.bfloat16),
        in_specs=[
            pl.BlockSpec((rows, 1), lambda n: (0, 0)),
            pl.BlockSpec((1, rows), lambda n: (0, 0)),
            column,
            column,
            column,
        ],
        out_specs=pl.BlockSpec((units, count, total, 3 * HD), lambda n: (0, n, 0, 0)),
        scratch_shapes=[
            pltpu.VMEM((units * total, rows), jnp.bfloat16),
            pltpu.VMEM((units * total, 3 * HD), jnp.bfloat16),
        ],
        compiler_params=pltpu.CompilerParams(vmem_limit_bytes=VMEM_LIMIT),
        cost_estimate=pl.CostEstimate(
            flops=2 * units * span * total * rows * 3 * HD,
            bytes_accessed=2 * 3 * HD * span * (rows + units * total),
            transcendentals=0,
        ),
        name="sort_rows",
    )(target_row.reshape(rows, 1), target_row.reshape(1, rows), queries, keys, values)
    return sent.reshape(units * span, total, 3 * HD)


def plan_kernel(devices, span, rows, total, win, *refs):
    piece_refs, (offset_ref, place_ref, crowded_ref) = refs[:-3], refs[-3:]
    lines = []
    for ref in piece_refs:
        tail = ref[...].astype(jnp.float32).reshape(-1, SUB, 3 * HD)
        lines += [tail[n, SUB - 3 :, :] for n in range(tail.shape[0])]
    high = jnp.concatenate([line[0:1] for line in lines], axis=0)
    low = jnp.concatenate([line[1:2] for line in lines], axis=0)
    crowded = jnp.concatenate([line[2:3] for line in lines], axis=0)
    crowded_ref[...] = jnp.max(jnp.max(crowded, axis=1, keepdims=True), axis=0, keepdims=True).astype(jnp.int32)
    place = jnp.where(high > 0.0, (high - 1.0) * BASE + low, -1.0).astype(jnp.int32)
    per = max(HD // win, 1)
    groups = devices // per
    wide = per * win
    lane = lax.broadcasted_iota(jnp.int32, (groups, wide), 1)
    shifted = {}
    for t in range((total - win) // SUB + 1):
        for e in range(per):
            turn = (e * win - SUB * t) % (3 * HD)
            part = place[e * groups : (e + 1) * groups]
            shifted[t, e] = (pltpu.roll(part, turn, 1) if turn else part)[:, :wide]
    for d in range(span):
        begun = jnp.sum(jnp.where((place >= 0) & (place < d * rows), 1, 0), axis=1, keepdims=True)
        offset = jnp.minimum(begun // SUB * SUB, total - win)
        offset_ref[d] = jnp.broadcast_to(offset, (devices, HD))
        out = jnp.full((groups, wide), -1, jnp.int32)
        for (t, e), part in shifted.items():
            mine = (offset[e * groups : (e + 1) * groups] == SUB * t) & (lane >= e * win) & (lane < (e + 1) * win)
            out = jnp.where(mine, part, out)
        place_ref[d] = out


def plan_rows(received, devices, span, rows, total, win):
    wide = max(HD // win, 1) * win
    groups = devices * win // wide
    last = total // SUB - 1
    in_specs = []
    for piece in received:
        if piece.ndim == 2:
            in_specs.append(pl.BlockSpec((SUB, 3 * HD), lambda n: (last, 0)))
        else:
            in_specs.append(pl.BlockSpec((piece.shape[0], SUB, 3 * HD), lambda n: (0, last, 0)))
    offsets, places, crowded = pl.pallas_call(
        functools.partial(plan_kernel, devices, span, rows, total, win),
        grid=(1,),
        out_shape=[
            jax.ShapeDtypeStruct((span, devices, HD), jnp.int32),
            jax.ShapeDtypeStruct((span, groups, wide), jnp.int32),
            jax.ShapeDtypeStruct((1, 1), jnp.int32),
        ],
        in_specs=in_specs,
        out_specs=[
            pl.BlockSpec((span, devices, HD), lambda n: (0, 0, 0)),
            pl.BlockSpec((span, groups, wide), lambda n: (0, 0, 0)),
            pl.BlockSpec((1, 1), lambda n: (0, 0)),
        ],
        compiler_params=pltpu.CompilerParams(vmem_limit_bytes=VMEM_LIMIT),
        name="plan_rows",
    )(*received)
    return offsets[:, :, 0].reshape(-1), places, crowded[0, 0] > 0


def attend_kernel(
    count, rows, span, win, block,
    own_ref, offset_ref, low_ref, high_ref, place_ref, first_ref, *refs,
):
    sources = [ref if len(ref.shape) == 2 else ref.at[n]
               for ref in refs[:count] for n in range(1 if len(ref.shape) == 2 else ref.shape[0])]
    out_refs = refs[-11 - span : -11]
    q_all, k_all, v_all, window, begins, top, mixed, scores, weights, fades, totals = refs[-11:]
    devices = len(sources)
    groups, wide = place_ref.shape[1:]
    per = wide // win
    blocks = span * rows // block
    lanes = [slice(n * HD, (n + 1) * HD) for n in range(block // HD)]
    part = min(64, block)

    for n in range(span * rows // HD):
        begin = jnp.broadcast_to(first_ref[n : n + 1, :], (HD, HD))
        begins[n * HD : (n + 1) * HD, :] = jnp.transpose(begin)

    def place_block(d, carry):
        for p in range(groups):
            for e in range(per):
                i = e * groups + p
                offset = pl.multiple_of(offset_ref[d * devices + i], SUB)
                slot = p * wide + e * win
                window[slot : slot + win, :] = sources[i][pl.ds(offset, win), :]
        base = pl.multiple_of(d * rows, SUB)
        position = lax.broadcasted_iota(jnp.int32, (rows, wide), 0) + base
        onehot = [
            jnp.where(position == place_ref[d, p : p + 1, :], 1.0, 0.0).astype(jnp.bfloat16)
            for p in range(groups)
        ]
        onehot = jnp.concatenate(onehot, axis=1) if groups > 1 else onehot[0]
        placed = jnp.dot(onehot, window[...], preferred_element_type=jnp.float32)
        scaled = placed[:, :HD] * EXP2_SCALE
        high = scaled.astype(jnp.bfloat16)
        q_all[pl.ds(base, rows), :HD] = high
        q_all[pl.ds(base, rows), HD:] = (scaled - high.astype(jnp.float32)).astype(jnp.bfloat16)
        key = placed[:, HD : 2 * HD].astype(jnp.bfloat16)
        k_all[pl.ds(base, rows), :HD] = key
        k_all[pl.ds(base, rows), HD:] = key
        v_all[pl.ds(base, rows), :HD] = placed[:, 2 * HD :].astype(jnp.bfloat16)
        return carry

    lax.fori_loop(0, span, place_block, 0)

    def starting(index):
        return pl.multiple_of(index * block, block)

    def score(i, j, slot):
        scores[slot][...] = lax.dot_general(
            q_all[pl.ds(starting(i), block), :],
            k_all[pl.ds(starting(j), block), :],
            (((1,), (1,)), ((), ())),
            preferred_element_type=jnp.float32,
        )

    def mix(j, slot):
        mixed[...] = mixed[...] * fades[slot][...] + jnp.dot(
            weights[slot][...], v_all[pl.ds(starting(j), block), :HD], preferred_element_type=jnp.float32
        )

    def weigh(i, j, fresh, slot, diagonal, bounded):
        lane = lax.broadcasted_iota(jnp.int32, (part, HD), 1)
        down = lax.broadcasted_iota(jnp.int32, (part, HD), 0)
        for r in range(0, block, part):
            here = slice(r, r + part)
            if bounded:
                begin = begins[pl.ds(pl.multiple_of(i * block + r, part), part), :] - starting(j) - lane
            columns = []
            for n, cols in enumerate(lanes):
                if diagonal and n * HD >= r + part:
                    break
                raw = scores[slot][here, cols]
                if bounded:
                    raw = jnp.where(begin <= n * HD, raw, NEG)
                if diagonal and (n + 1) * HD > r + 1:
                    raw = jnp.where(lane - down <= r - n * HD, raw, NEG)
                columns.append(raw)
            peak = functools.reduce(jnp.maximum, columns)
            old = jnp.where(fresh, NEG, top[here, :])
            new = jnp.maximum(old, jnp.max(peak, axis=1, keepdims=True))
            fade = jnp.exp2(old - new)
            total = totals[1 - slot][here, :] * fade
            for n, cols in enumerate(lanes):
                if n < len(columns):
                    weight = jnp.exp2(columns[n] - new)
                    total += weight
                    weights[slot][here, cols] = weight.astype(jnp.bfloat16)
                else:
                    weights[slot][here, cols] = jnp.zeros((part, HD), jnp.bfloat16)
            top[here, :] = new
            fades[slot][here, :] = fade
            totals[slot][here, :] = total

    def finish(i, slot):
        total = jnp.sum(totals[slot][...], axis=1, keepdims=True)
        v_all[pl.ds(starting(i), block), HD:] = (mixed[...] / total).astype(jnp.bfloat16)

    def step(state, slot):
        last_i, last_j, i, j = state
        done = j == i
        next_i = jnp.where(done, jnp.minimum(i + 1, blocks - 1), i)
        next_j = jnp.where(done, low_ref[next_i], j + 1)
        bounded = high_ref[i] > j * block
        fresh = j == low_ref[i]

        def work(diagonal, bounded):
            mix(last_j, 1 - slot)
            score(next_i, next_j, 1 - slot)
            weigh(i, j, fresh, slot, diagonal, bounded)

        @pl.when(done)
        def _():
            work(True, True)

        @pl.when(jnp.logical_not(done) & bounded)
        def _():
            work(False, True)

        @pl.when(jnp.logical_not(done | bounded))
        def _():
            work(False, False)

        @pl.when(last_j == last_i)
        def _():
            finish(last_i, 1 - slot)

        return i, j, next_i, next_j

    pairs = blocks * (blocks + 1) // 2
    for i in range(blocks):
        pairs -= low_ref[i]
    mixed[...] = jnp.zeros_like(mixed)
    for slot in range(2):
        weights[slot][...] = jnp.zeros_like(weights[slot])
        fades[slot][...] = jnp.zeros_like(fades[slot])
        totals[slot][...] = jnp.zeros_like(totals[slot])
    top[...] = jnp.full_like(top, NEG)
    score(0, 0, 0)

    def two_steps(n, state):
        middle = step(state, 0)
        after = step_if(2 * n + 1 < pairs, middle)
        return after

    def step_if(more, state):
        _, _, i, j = state
        done = j == i
        next_i = jnp.where(done, jnp.minimum(i + 1, blocks - 1), i)
        next_j = jnp.where(done, low_ref[next_i], j + 1)

        @pl.when(more)
        def _():
            step(state, 1)

        return i, j, next_i, next_j

    zero = jnp.int32(0)
    lax.fori_loop(0, (pairs + 1) // 2, two_steps, (zero + 1, zero, zero, zero))

    for slot in range(2):

        @pl.when(pairs % 2 == 1 - slot)
        def _():
            mix(blocks - 1, slot)
            finish(blocks - 1, slot)

    for k in range(span):
        owner = lax.rem(own_ref[1] + k, span)
        out_refs[k][...] = v_all[pl.ds(pl.multiple_of(owner * rows, SUB), rows), HD:]


def attend(received, after, own, offsets, places, first, rows, span, win):
    total = received[0].shape[-2]
    devices = sum(piece.size for piece in received) // (total * 3 * HD)
    length = span * rows
    block = math.gcd(length, 512)
    low = first[::block] // block
    high = first[block - 1 :: block]
    vmem = pl.BlockSpec(memory_space=pltpu.VMEM)
    smem = pl.BlockSpec(memory_space=pltpu.SMEM)
    narrow = pltpu.VMEM((block, HD), jnp.float32)
    return pl.pallas_call(
        functools.partial(attend_kernel, len(received), rows, span, win, block),
        out_shape=[jax.ShapeDtypeStruct((rows, HD), jnp.bfloat16)] * span,
        in_specs=[smem] * 4 + [vmem] * (2 + len(received)) + [pl.BlockSpec(memory_space=pl.ANY)] * len(after),
        out_specs=[vmem] * span,
        scratch_shapes=[
            pltpu.VMEM((length, 2 * HD), jnp.bfloat16),
            pltpu.VMEM((length, 2 * HD), jnp.bfloat16),
            pltpu.VMEM((length, 2 * HD), jnp.bfloat16),
            pltpu.VMEM((devices * win, 3 * HD), jnp.bfloat16),
            pltpu.VMEM((length, HD), jnp.int32),
            narrow,
            narrow,
            [pltpu.VMEM((block, block), jnp.float32)] * 2,
            [pltpu.VMEM((block, block), jnp.bfloat16)] * 2,
            [narrow] * 2,
            [narrow] * 2,
        ],
        compiler_params=pltpu.CompilerParams(vmem_limit_bytes=VMEM_LIMIT),
        cost_estimate=pl.CostEstimate(
            flops=2 * length * devices * win * 3 * HD + 8 * length * length * HD,
            bytes_accessed=2 * (devices * total * 3 * HD + length * HD),
            transcendentals=length * length // 2,
        ),
        name="attend_head",
    )(own, offsets, low, high, places, first.reshape(length // HD, HD), *received, *after)


def join_kernel(span, own_ref, *refs):
    out_ref = refs[-1]
    for n, ref in enumerate(refs[:-1]):
        head = n // span * span + lax.rem(own_ref[1] + span - n % span, span)
        out_ref[:, pl.ds(pl.multiple_of(head * HD, HD), HD)] = ref[...]


def join_heads(own, pieces, span):
    vmem = pl.BlockSpec(memory_space=pltpu.VMEM)
    smem = pl.BlockSpec(memory_space=pltpu.SMEM)
    rows = pieces[0].shape[0]
    return pl.pallas_call(
        functools.partial(join_kernel, span),
        out_shape=jax.ShapeDtypeStruct((rows, len(pieces) * HD), jnp.bfloat16),
        in_specs=[smem] + [vmem] * len(pieces),
        out_specs=vmem,
        compiler_params=pltpu.CompilerParams(vmem_limit_bytes=VMEM_LIMIT),
        name="join_heads",
    )(own, *pieces)


def body(queries, keys, values, target_row, doc_lengths):
    rows, width = queries.shape
    group = width // HD
    devices = lax.axis_size("seq")
    span = max(group // 2, 1)
    units = devices // span
    each = group // span
    length = span * rows
    pair_most = 3 * rows // (2 * devices)
    mean = rows // units
    most = min(pair_most * span, rows)
    usual = min(mean + mean // 16, most)
    index = lax.axis_index("seq")
    own = jnp.stack([index // span, index % span]).astype(jnp.int32)
    unit_start = index // span * length

    docs = jnp.arange(doc_lengths.shape[0])
    starts = jnp.sum(jnp.where(docs[:, None] < docs[None, :], doc_lengths[:, None], 0), axis=0)
    positions = unit_start + jnp.arange(length, dtype=jnp.int32)
    first = jnp.max(jnp.where(starts[None, :] <= positions[:, None], starts[None, :], 0), axis=1)
    first = jnp.maximum(first - unit_start, 0)

    def homeward(piece, shift):
        if shift == 0:
            return piece
        route = [
            (u * span + m, u * span + (m + shift) % span) for u in range(units) for m in range(span)
        ]
        return lax.ppermute(piece, "seq", route)

    def attended(cap):
        total = rounded_up(cap + 3, SUB)
        win = SUB
        while win < pair_most + SUB - 1:
            win *= 2
        win = min(total, win)
        pieces = []
        after = []
        for chunk in range(each):
            sent = sort_rows(queries, keys, values, target_row, units, span, cap, total, chunk)
            received = [lax.all_to_all(sent, "seq", split_axis=0, concat_axis=0, tiled=True)]
            if chunk == 0:
                offsets, places, crowded = plan_rows(received, devices, span, rows, total, win)
            heads = attend(received, after, own, offsets, places, first, rows, span, win)
            after = [homeward(heads[shift], shift) for shift in range(span)]
            pieces += after
        return pieces, crowded

    pieces, crowded = attended(usual)
    if usual == most:
        return join_heads(own, pieces, span)
    return lax.cond(
        crowded,
        lambda: join_heads(own, attended(most)[0], span),
        lambda: join_heads(own, pieces, span),
    )


def solution(mesh):
    in_specs = (P("seq", "head"), P("seq", "head"), P("seq", "head"), P("seq"), P())
    out_specs = P("seq", "head")
    return jax.shard_map(body, mesh=mesh, in_specs=in_specs, out_specs=out_specs, check_vma=False)
```

```python
import functools
import math

import jax
import jax.numpy as jnp
from jax import lax
from jax.experimental import pallas as pl
from jax.experimental.pallas import tpu as pltpu
from jax.sharding import PartitionSpec as P

HD = 128
SUB = 16
BASE = 64
NEG = -1e30
EXP2_SCALE = math.log2(math.e) / math.sqrt(HD)
VMEM_LIMIT = 40 * 1024 * 1024


def rounded_up(count, multiple):
    return -(-count // multiple) * multiple


def sort_kernel(units, span_rows, cap, total, target_col_ref, target_row_ref, q_ref, k_ref, v_ref, out_ref, onehot, notes, staged, sems):
    rows = q_ref.shape[0]
    lanes = 3 * HD

    @pl.when(pl.program_id(0) == 0)
    def _():
        across = target_row_ref[...]
        down = target_col_ref[...]
        unit = jnp.zeros_like(across)
        for u in range(1, units):
            unit += (across >= u * span_rows).astype(jnp.int32)
        inner = across - unit * span_rows
        before = (down < across) & (down >= unit * span_rows)
        place = jnp.sum(before.astype(jnp.int32), axis=0, keepdims=True)
        slot = jnp.where(place < cap, unit * total + place, -1)
        slots = lax.broadcasted_iota(jnp.int32, (units * total, rows), 0)
        onehot[...] = jnp.where(slots == slot, 1.0, 0.0).astype(jnp.bfloat16)
        crowded = jnp.max(jnp.where(place >= cap, 1.0, 0.0), axis=1, keepdims=True)
        high = inner // BASE
        kind = lax.broadcasted_iota(jnp.int32, (SUB, rows), 0)
        digits = jnp.where(kind == 0, high + 1, jnp.where(kind == 1, inner - high * BASE, 0))
        digits = digits.astype(jnp.float32).astype(jnp.bfloat16)
        spread = lax.broadcasted_iota(jnp.int32, (lanes, rows), 0)
        line = lax.broadcasted_iota(jnp.int32, (total, lanes), 0)
        for u in range(units):
            mine = jnp.where((spread == place) & (unit == u), 1.0, 0.0).astype(jnp.bfloat16)
            along = lax.dot_general(
                digits, mine, (((1,), (1,)), ((), ())), preferred_element_type=jnp.float32
            )
            note = jnp.where(line == total - 3, along[0:1], jnp.where(line == total - 2, along[1:2], 0.0))
            note = jnp.where(line == total - 1, crowded, note)
            notes[u * total : (u + 1) * total, :] = note.astype(jnp.bfloat16)

    count = q_ref.shape[1] // HD
    first = pl.program_id(0) * count

    def leaving(m):
        return pltpu.make_async_copy(staged.at[:, m], out_ref.at[:, first + m], sems.at[m])

    for m in range(count):

        @pl.when(pl.program_id(0) > 0)
        def _():
            leaving(m).wait()

        cols = slice(m * HD, (m + 1) * HD)
        block = jnp.concatenate([q_ref[:, cols], k_ref[:, cols], v_ref[:, cols]], axis=1)
        sent = jnp.dot(onehot[...], block, preferred_element_type=jnp.float32).astype(jnp.bfloat16)
        staged[:, m] = (sent + notes[...]).reshape(units, total, lanes)
        leaving(m).start()

    @pl.when(pl.program_id(0) == pl.num_programs(0) - 1)
    def _():
        for m in range(count):
            leaving(m).wait()


def sort_rows(queries, keys, values, target_row, units, span, cap, total, chunk):
    rows = queries.shape[0]
    steps = math.gcd(span, 2)
    count = span // steps
    column = pl.BlockSpec((rows, count * HD), lambda n: (0, chunk * steps + n))
    sent = pl.pallas_call(
        functools.partial(sort_kernel, units, span * rows, cap, total),
        grid=(steps,),
        out_shape=jax.ShapeDtypeStruct((units, span, total, 3 * HD), jnp.bfloat16),
        in_specs=[
            pl.BlockSpec((rows, 1), lambda n: (0, 0)),
            pl.BlockSpec((1, rows), lambda n: (0, 0)),
            column,
            column,
            column,
        ],
        out_specs=pl.BlockSpec(memory_space=pltpu.HBM),
        scratch_shapes=[
            pltpu.VMEM((units * total, rows), jnp.bfloat16),
            pltpu.VMEM((units * total, 3 * HD), jnp.bfloat16),
            pltpu.VMEM((units, count, total, 3 * HD), jnp.bfloat16),
            pltpu.SemaphoreType.DMA((count,)),
        ],
        compiler_params=pltpu.CompilerParams(vmem_limit_bytes=VMEM_LIMIT),
        cost_estimate=pl.CostEstimate(
            flops=2 * units * span * total * rows * 3 * HD,
            bytes_accessed=2 * 3 * HD * span * (rows + units * total),
            transcendentals=0,
        ),
        name="sort_rows",
    )(target_row.reshape(rows, 1), target_row.reshape(1, rows), queries, keys, values)
    return sent.reshape(units * span, total, 3 * HD)


def plan_kernel(devices, span, rows, total, win, *refs):
    tail_ref, offset_ref, place_ref, crowded_ref = refs
    tail = tail_ref[...].astype(jnp.float32)
    lines = [tail[n, SUB - 3 :, :] for n in range(devices)]
    high = jnp.concatenate([line[0:1] for line in lines], axis=0)
    low = jnp.concatenate([line[1:2] for line in lines], axis=0)
    crowded = jnp.concatenate([line[2:3] for line in lines], axis=0)
    crowded_ref[...] = jnp.max(jnp.max(crowded, axis=1, keepdims=True), axis=0, keepdims=True).astype(jnp.int32)
    place = jnp.where(high > 0.0, (high - 1.0) * BASE + low, -1.0).astype(jnp.int32)
    per = max(HD // win, 1)
    groups = devices // per
    wide = per * win
    lane = lax.broadcasted_iota(jnp.int32, (groups, wide), 1)
    shifted = {}
    for t in range((total - win) // SUB + 1):
        for e in range(per):
            turn = (e * win - SUB * t) % (3 * HD)
            part = place[e * groups : (e + 1) * groups]
            shifted[t, e] = (pltpu.roll(part, turn, 1) if turn else part)[:, :wide]
    for d in range(span):
        begun = jnp.sum(jnp.where((place >= 0) & (place < d * rows), 1, 0), axis=1, keepdims=True)
        offset = jnp.minimum(begun // SUB * SUB, total - win)
        offset_ref[d] = jnp.broadcast_to(offset, (devices, HD))
        out = jnp.full((groups, wide), -1, jnp.int32)
        for (t, e), part in shifted.items():
            mine = (offset[e * groups : (e + 1) * groups] == SUB * t) & (lane >= e * win) & (lane < (e + 1) * win)
            out = jnp.where(mine, part, out)
        place_ref[d] = out


def plan_rows(received, devices, span, rows, total, win):
    wide = max(HD // win, 1) * win
    groups = devices * win // wide
    last = total // SUB - 1
    offsets, places, crowded = pl.pallas_call(
        functools.partial(plan_kernel, devices, span, rows, total, win),
        grid=(1,),
        out_shape=[
            jax.ShapeDtypeStruct((span, devices, HD), jnp.int32),
            jax.ShapeDtypeStruct((span, groups, wide), jnp.int32),
            jax.ShapeDtypeStruct((1, 1), jnp.int32),
        ],
        in_specs=[pl.BlockSpec((devices, SUB, 3 * HD), lambda n: (0, last, 0))],
        out_specs=[
            pl.BlockSpec((span, devices, HD), lambda n: (0, 0, 0)),
            pl.BlockSpec((span, groups, wide), lambda n: (0, 0, 0)),
            pl.BlockSpec((1, 1), lambda n: (0, 0)),
        ],
        compiler_params=pltpu.CompilerParams(vmem_limit_bytes=VMEM_LIMIT),
        name="plan_rows",
    )(received)
    return offsets[:, :, 0].reshape(-1), places, crowded[0, 0] > 0


def attend_kernel(
    rows, span, win, block,
    own_ref, offset_ref, low_ref, high_ref, place_ref, first_ref, *refs,
):
    out_refs = refs[-13 - span : -13]
    received, arrival, q_all, k_all, v_all, o_all, window, top, mixed, scores, weights, fades, totals = refs[-13:]
    devices = received.shape[0]
    groups, wide = place_ref.shape[1:]
    per = wide // win
    blocks = span * rows // block
    lanes = [slice(n, n + HD) for n in range(0, block, HD)]
    copy = pltpu.make_async_copy(refs[0], received, arrival)
    copy.start()
    mixed[...] = jnp.zeros_like(mixed)
    for slot in range(2):
        weights[slot][...] = jnp.zeros_like(weights[slot])
        fades[slot][...] = jnp.zeros_like(fades[slot])
        totals[slot][...] = jnp.zeros_like(totals[slot])
    top[...] = jnp.full_like(top, NEG)
    copy.wait()

    def place_block(d, carry):
        for p in range(groups):
            for e in range(per):
                i = e * groups + p
                offset = pl.multiple_of(offset_ref[d * devices + i], SUB)
                slot = p * wide + e * win
                window[slot : slot + win, :] = received[i, pl.ds(offset, win), :]
        base = pl.multiple_of(d * rows, HD)
        position = lax.broadcasted_iota(jnp.int32, (rows, wide), 0) + base
        onehot = [
            jnp.where(position == place_ref[d, p : p + 1, :], 1.0, 0.0).astype(jnp.bfloat16)
            for p in range(groups)
        ]
        onehot = jnp.concatenate(onehot, axis=1) if groups > 1 else onehot[0]
        placed = jnp.dot(onehot, window[...], preferred_element_type=jnp.float32)
        scaled = placed[:, :HD] * EXP2_SCALE
        high = scaled.astype(jnp.bfloat16)
        q_all[pl.ds(base, rows), :HD] = high
        q_all[pl.ds(base, rows), HD:] = (scaled - high.astype(jnp.float32)).astype(jnp.bfloat16)
        key = placed[:, HD : 2 * HD].astype(jnp.bfloat16)
        k_all[pl.ds(base, rows), :HD] = key
        k_all[pl.ds(base, rows), HD:] = key
        v_all[:, pl.ds(base, rows)] = jnp.transpose(placed[:, 2 * HD :]).astype(jnp.bfloat16)
        return carry

    lax.fori_loop(0, span, place_block, 0)

    def starting(index):
        return pl.multiple_of(index * block, block)

    def score(i, j, slot):
        scores[slot][...] = lax.dot_general(
            k_all[pl.ds(starting(j), block), :],
            q_all[pl.ds(starting(i), block), :],
            (((1,), (1,)), ((), ())),
            preferred_element_type=jnp.float32,
        )

    def mix(j, slot):
        mixed[...] = mixed[...] * fades[slot][...] + jnp.dot(
            v_all[:, pl.ds(starting(j), block)], weights[slot][...], preferred_element_type=jnp.float32
        )

    def weigh(i, j, fresh, slot, diagonal, bounded):
        down = lax.broadcasted_iota(jnp.int32, (HD, HD), 0)
        lane = lax.broadcasted_iota(jnp.int32, (HD, HD), 1)
        for c, cols in enumerate(lanes):
            if bounded:
                begin = first_ref[pl.ds(i * len(lanes) + c, 1), :] - starting(j)

            def raw(n):
                part = scores[slot][lanes[n], cols]
                if bounded:
                    part = jnp.where(down >= begin - n * HD, part, NEG)
                if diagonal and n == c:
                    part = jnp.where(down <= lane, part, NEG)
                return part

            seen = range(c + 1) if diagonal else range(len(lanes))
            peak = functools.reduce(jnp.maximum, [raw(n) for n in seen])
            old = jnp.where(fresh, NEG, top[:, cols])
            new = jnp.maximum(old, jnp.max(peak, axis=0, keepdims=True))
            fade = jnp.exp2(old - new)
            total = None
            for n in range(len(lanes)):
                if n in seen:
                    weight = jnp.exp2(raw(n) - new)
                    total = weight if total is None else total + weight
                    weights[slot][lanes[n], cols] = weight.astype(jnp.bfloat16)
                else:
                    weights[slot][lanes[n], cols] = jnp.zeros((HD, HD), jnp.bfloat16)
            top[:, cols] = new
            fades[slot][:, cols] = fade
            totals[slot][:, cols] = totals[1 - slot][:, cols] * fade + jnp.sum(total, axis=0, keepdims=True)

    def finish(i, slot):
        result = mixed[...] / totals[slot][...]
        o_all[pl.ds(starting(i), block), :] = jnp.transpose(result).astype(jnp.bfloat16)

    def following(i, j):
        done = j == i
        next_i = jnp.where(done, jnp.minimum(i + 1, blocks - 1), i)
        return next_i, jnp.where(done, low_ref[next_i], j + 1)

    def step(state, slot):
        last_i, last_j, i, j = state
        next_i, next_j = following(i, j)
        done = j == i
        bounded = high_ref[i] > j * block
        fresh = j == low_ref[i]

        def work(diagonal, bounded):
            mix(last_j, 1 - slot)
            score(next_i, next_j, 1 - slot)
            weigh(i, j, fresh, slot, diagonal, bounded)

        @pl.when(done)
        def _():
            work(True, True)

        @pl.when(jnp.logical_not(done) & bounded)
        def _():
            work(False, True)

        @pl.when(jnp.logical_not(done | bounded))
        def _():
            work(False, False)

        @pl.when(last_j == last_i)
        def _():
            finish(last_i, 1 - slot)

        return i, j, next_i, next_j

    pairs = blocks * (blocks + 1) // 2
    for i in range(blocks):
        pairs -= low_ref[i]
    score(0, 0, 0)

    def two_steps(n, state):
        state = step(state, 0)
        _, _, i, j = state

        @pl.when(2 * n + 1 < pairs)
        def _():
            step(state, 1)

        return i, j, *following(i, j)

    zero = jnp.int32(0)
    lax.fori_loop(0, (pairs + 1) // 2, two_steps, (zero + 1, zero, zero, zero))

    for slot in range(2):

        @pl.when(pairs % 2 == 1 - slot)
        def _():
            mix(blocks - 1, slot)
            finish(blocks - 1, slot)

    for k in range(span):
        owner = lax.rem(own_ref[1] + k, span)
        out_refs[k][...] = o_all[pl.ds(pl.multiple_of(owner * rows, SUB), rows), :]


def attend(received, after, own, offsets, places, first, rows, span, win):
    devices, total, _ = received.shape
    length = span * rows
    block = math.gcd(length, 512)
    low = first[::block] // block
    high = first[block - 1 :: block]
    vmem = pl.BlockSpec(memory_space=pltpu.VMEM)
    smem = pl.BlockSpec(memory_space=pltpu.SMEM)
    anywhere = pl.BlockSpec(memory_space=pl.ANY)
    line = pltpu.VMEM((1, block), jnp.float32)
    return pl.pallas_call(
        functools.partial(attend_kernel, rows, span, win, block),
        out_shape=[jax.ShapeDtypeStruct((rows, HD), jnp.bfloat16)] * span,
        in_specs=[smem] * 4 + [vmem] * 2 + [anywhere] * (1 + len(after)),
        out_specs=[vmem] * span,
        scratch_shapes=[
            pltpu.VMEM(received.shape, jnp.bfloat16),
            pltpu.SemaphoreType.DMA,
            pltpu.VMEM((length, 2 * HD), jnp.bfloat16),
            pltpu.VMEM((length, 2 * HD), jnp.bfloat16),
            pltpu.VMEM((HD, length), jnp.bfloat16),
            pltpu.VMEM((length, HD), jnp.bfloat16),
            pltpu.VMEM((devices * win, 3 * HD), jnp.bfloat16),
            line,
            pltpu.VMEM((HD, block), jnp.float32),
            [pltpu.VMEM((block, block), jnp.float32)] * 2,
            [pltpu.VMEM((block, block), jnp.bfloat16)] * 2,
            [line] * 2,
            [line] * 2,
        ],
        compiler_params=pltpu.CompilerParams(vmem_limit_bytes=VMEM_LIMIT),
        cost_estimate=pl.CostEstimate(
            flops=2 * length * devices * win * 3 * HD + 8 * length * length * HD,
            bytes_accessed=2 * (devices * total * 3 * HD + length * HD),
            transcendentals=length * length // 2,
        ),
        name="attend_head",
    )(own, offsets, low, high, places, first.reshape(length // HD, HD), received, *after)


def join_kernel(span, own_ref, *refs):
    out_ref = refs[-1]
    for n, ref in enumerate(refs[:-1]):
        head = n // span * span + lax.rem(own_ref[1] + span - n % span, span)
        out_ref[:, pl.ds(pl.multiple_of(head * HD, HD), HD)] = ref[...]


def join_heads(own, pieces, span):
    vmem = pl.BlockSpec(memory_space=pltpu.VMEM)
    smem = pl.BlockSpec(memory_space=pltpu.SMEM)
    rows = pieces[0].shape[0]
    return pl.pallas_call(
        functools.partial(join_kernel, span),
        out_shape=jax.ShapeDtypeStruct((rows, len(pieces) * HD), jnp.bfloat16),
        in_specs=[smem] + [vmem] * len(pieces),
        out_specs=vmem,
        compiler_params=pltpu.CompilerParams(vmem_limit_bytes=VMEM_LIMIT),
        name="join_heads",
    )(own, *pieces)


def body(queries, keys, values, target_row, doc_lengths):
    rows, width = queries.shape
    group = width // HD
    devices = lax.axis_size("seq")
    span = max(group // 2, 1)
    units = devices // span
    each = group // span
    length = span * rows
    pair_most = 3 * rows // (2 * devices)
    mean = rows // units
    most = min(pair_most * span, rows)
    usual = min(mean + mean // 16, most)
    index = lax.axis_index("seq")
    own = jnp.stack([index // span, index % span]).astype(jnp.int32)
    unit_start = index // span * length

    docs = jnp.arange(doc_lengths.shape[0])
    starts = jnp.sum(jnp.where(docs[:, None] < docs[None, :], doc_lengths[:, None], 0), axis=0)
    positions = unit_start + jnp.arange(length, dtype=jnp.int32)
    first = jnp.max(jnp.where(starts[None, :] <= positions[:, None], starts[None, :], 0), axis=1)
    first = jnp.maximum(first - unit_start, 0)

    def homeward(piece, shift):
        if shift == 0:
            return piece
        route = [
            (u * span + m, u * span + (m + shift) % span) for u in range(units) for m in range(span)
        ]
        return lax.ppermute(piece, "seq", route)

    def attended(cap):
        total = rounded_up(cap + 3, SUB)
        win = SUB
        while win < pair_most + SUB - 1:
            win *= 2
        win = min(total, win)
        pieces = []
        after = []
        for chunk in range(each):
            sent = sort_rows(queries, keys, values, target_row, units, span, cap, total, chunk)
            received = lax.all_to_all(sent, "seq", split_axis=0, concat_axis=0, tiled=True)
            if chunk == 0:
                offsets, places, crowded = plan_rows(received, devices, span, rows, total, win)
            heads = attend(received, after, own, offsets, places, first, rows, span, win)
            after = [homeward(heads[shift], shift) for shift in range(span)]
            pieces += after
        return pieces, crowded

    pieces, crowded = attended(usual)
    if usual == most:
        return join_heads(own, pieces, span)
    return lax.cond(
        crowded,
        lambda: join_heads(own, attended(most)[0], span),
        lambda: join_heads(own, pieces, span),
    )


def solution(mesh):
    in_specs = (P("seq", "head"), P("seq", "head"), P("seq", "head"), P("seq"), P())
    out_specs = P("seq", "head")
    return jax.shard_map(body, mesh=mesh, in_specs=in_specs, out_specs=out_specs, check_vma=False)
```

```python
import functools
import math

import jax
import jax.numpy as jnp
from jax import lax
from jax.experimental import pallas as pl
from jax.experimental.pallas import tpu as pltpu
from jax.sharding import PartitionSpec as P

HD = 128
SUB = 16
BASE = 64
QUEUED = 5
NEG = -1e30
EXP2_SCALE = math.log2(math.e) / math.sqrt(HD)
VMEM_LIMIT = 40 * 1024 * 1024
SORT_LIMIT = 60 * 1024 * 1024


def rounded_up(count, multiple):
    return -(-count // multiple) * multiple


def fill(units, span_rows, cap, total, target_ref, onehot, notes):
    rows = onehot.shape[1]
    lanes = 3 * HD
    across = jnp.concatenate([target_ref[n : n + 1, :] for n in range(rows // HD)], axis=1)
    down = jnp.concatenate(
        [
            jnp.transpose(jnp.broadcast_to(target_ref[n : n + 1, :], (HD, HD)))
            for n in range(rows // HD)
        ],
        axis=0,
    )
    down = jnp.concatenate([down] * (rows // HD), axis=1)
    unit = jnp.zeros_like(across)
    for u in range(1, units):
        unit += (across >= u * span_rows).astype(jnp.int32)
    inner = across - unit * span_rows
    before = (down < across) & (down >= unit * span_rows)
    place = jnp.sum(before.astype(jnp.int32), axis=0, keepdims=True)
    slot = jnp.where(place < cap, unit * total + place, -1)
    slots = lax.broadcasted_iota(jnp.int32, (units * total, rows), 0)
    onehot[...] = jnp.where(slots == slot, 1.0, 0.0).astype(jnp.bfloat16)
    crowded = jnp.max(jnp.where(place >= cap, 1.0, 0.0), axis=1, keepdims=True)
    high = inner // BASE
    kind = lax.broadcasted_iota(jnp.int32, (SUB, rows), 0)
    digits = jnp.where(kind == 0, high + 1, jnp.where(kind == 1, inner - high * BASE, 0))
    digits = digits.astype(jnp.float32).astype(jnp.bfloat16)
    spread = lax.broadcasted_iota(jnp.int32, (lanes, rows), 0)
    line = lax.broadcasted_iota(jnp.int32, (total, lanes), 0)
    for u in range(units):
        mine = jnp.where((spread == place) & (unit == u), 1.0, 0.0).astype(jnp.bfloat16)
        along = lax.dot_general(
            digits, mine, (((1,), (1,)), ((), ())), preferred_element_type=jnp.float32
        )
        note = jnp.where(line == total - 3, along[0:1], jnp.where(line == total - 2, along[1:2], 0.0))
        note = jnp.where(line == total - 1, crowded, note)
        notes[u * total : (u + 1) * total, :] = note.astype(jnp.bfloat16)


def sort_kernel(units, span_rows, cap, total, target_ref, q_ref, k_ref, v_ref, out_ref, onehot, notes):
    @pl.when(pl.program_id(0) == 0)
    def _():
        fill(units, span_rows, cap, total, target_ref, onehot, notes)

    for m in range(q_ref.shape[1] // HD):
        cols = slice(m * HD, (m + 1) * HD)
        block = jnp.concatenate([q_ref[:, cols], k_ref[:, cols], v_ref[:, cols]], axis=1)
        sent = jnp.dot(onehot[...], block, preferred_element_type=jnp.float32).astype(jnp.bfloat16)
        out_ref[:, m] = (sent + notes[...]).reshape(units, total, 3 * HD)


def sort_apart_kernel(units, span_rows, cap, total, shifts, own_ref, target_ref, q_ref, k_ref, v_ref, *refs):
    out_refs, onehot, notes = refs[:-2], refs[-2], refs[-1]
    fill(units, span_rows, cap, total, target_ref, onehot, notes)
    span = q_ref.shape[1] // HD
    for n, (a, b) in enumerate(shifts):
        member = lax.rem(own_ref[0] + b, span)
        unit = lax.rem(own_ref[1] + a, units)
        cols = pl.ds(pl.multiple_of(member * HD, HD), HD)
        part = pl.ds(pl.multiple_of(unit * total, SUB), total)
        block = jnp.concatenate([q_ref[:, cols], k_ref[:, cols], v_ref[:, cols]], axis=1)
        sent = jnp.dot(onehot[part, :], block, preferred_element_type=jnp.float32)
        out_refs[n][...] = sent.astype(jnp.bfloat16) + notes[part, :]


def sort_apart(queries, keys, values, target_row, own, units, span, cap, total, chunk, shifts):
    rows = queries.shape[0]
    column = pl.BlockSpec((rows, span * HD), lambda n: (0, chunk))
    return pl.pallas_call(
        functools.partial(sort_apart_kernel, units, span * rows, cap, total, shifts),
        grid=(1,),
        out_shape=[jax.ShapeDtypeStruct((total, 3 * HD), jnp.bfloat16)] * len(shifts),
        in_specs=[
            pl.BlockSpec(memory_space=pltpu.SMEM),
            pl.BlockSpec((rows // HD, HD), lambda n: (0, 0)),
            column,
            column,
            column,
        ],
        out_specs=[pl.BlockSpec((total, 3 * HD), lambda n: (0, 0))] * len(shifts),
        scratch_shapes=[
            pltpu.VMEM((units * total, rows), jnp.bfloat16),
            pltpu.VMEM((units * total, 3 * HD), jnp.bfloat16),
        ],
        compiler_params=pltpu.CompilerParams(vmem_limit_bytes=SORT_LIMIT),
        cost_estimate=pl.CostEstimate(
            flops=2 * len(shifts) * total * rows * 3 * HD,
            bytes_accessed=2 * 3 * HD * (span * rows + len(shifts) * total),
            transcendentals=0,
        ),
        name="sort_apart",
    )(own, target_row.reshape(rows // HD, HD), queries, keys, values)


def sort_rows(queries, keys, values, target_row, units, span, cap, total, chunk):
    rows = queries.shape[0]
    steps = math.gcd(span, 2)
    count = span // steps
    column = pl.BlockSpec((rows, count * HD), lambda n: (0, chunk * steps + n))
    sent = pl.pallas_call(
        functools.partial(sort_kernel, units, span * rows, cap, total),
        grid=(steps,),
        out_shape=jax.ShapeDtypeStruct((units, span, total, 3 * HD), jnp.bfloat16),
        in_specs=[
            pl.BlockSpec((rows // HD, HD), lambda n: (0, 0)),
            column,
            column,
            column,
        ],
        out_specs=pl.BlockSpec((units, count, total, 3 * HD), lambda n: (0, n, 0, 0)),
        scratch_shapes=[
            pltpu.VMEM((units * total, rows), jnp.bfloat16),
            pltpu.VMEM((units * total, 3 * HD), jnp.bfloat16),
        ],
        compiler_params=pltpu.CompilerParams(vmem_limit_bytes=SORT_LIMIT),
        cost_estimate=pl.CostEstimate(
            flops=2 * units * span * total * rows * 3 * HD,
            bytes_accessed=2 * 3 * HD * span * (rows + units * total),
            transcendentals=0,
        ),
        name="sort_rows",
    )(target_row.reshape(rows // HD, HD), queries, keys, values)
    return sent.reshape(units * span, total, 3 * HD)


def plan_kernel(devices, span, rows, total, win, *refs):
    tail_ref, offset_ref, place_ref, crowded_ref = refs
    tail = tail_ref[...].astype(jnp.float32)
    lines = [tail[n, SUB - 3 :, :] for n in range(devices)]
    high = jnp.concatenate([line[0:1] for line in lines], axis=0)
    low = jnp.concatenate([line[1:2] for line in lines], axis=0)
    crowded = jnp.concatenate([line[2:3] for line in lines], axis=0)
    crowded_ref[...] = jnp.max(jnp.max(crowded, axis=1, keepdims=True), axis=0, keepdims=True).astype(jnp.int32)
    place = jnp.where(high > 0.0, (high - 1.0) * BASE + low, -1.0).astype(jnp.int32)
    per = max(HD // win, 1)
    groups = devices // per
    wide = per * win
    lane = lax.broadcasted_iota(jnp.int32, (groups, wide), 1)
    shifted = {}
    for t in range((total - win) // SUB + 1):
        for e in range(per):
            turn = (e * win - SUB * t) % (3 * HD)
            part = place[e * groups : (e + 1) * groups]
            shifted[t, e] = (pltpu.roll(part, turn, 1) if turn else part)[:, :wide]
    for d in range(span):
        begun = jnp.sum(jnp.where((place >= 0) & (place < d * rows), 1, 0), axis=1, keepdims=True)
        offset = jnp.minimum(begun // SUB * SUB, total - win)
        offset_ref[d] = jnp.broadcast_to(offset, (devices, HD))
        out = jnp.full((groups, wide), -1, jnp.int32)
        for (t, e), part in shifted.items():
            mine = (offset[e * groups : (e + 1) * groups] == SUB * t) & (lane >= e * win) & (lane < (e + 1) * win)
            out = jnp.where(mine, part, out)
        place_ref[d] = out


def plan_rows(received, devices, span, rows, total, win):
    wide = max(HD // win, 1) * win
    groups = devices * win // wide
    last = total // SUB - 1
    offsets, places, crowded = pl.pallas_call(
        functools.partial(plan_kernel, devices, span, rows, total, win),
        grid=(1,),
        out_shape=[
            jax.ShapeDtypeStruct((span, devices, HD), jnp.int32),
            jax.ShapeDtypeStruct((span, groups, wide), jnp.int32),
            jax.ShapeDtypeStruct((1, 1), jnp.int32),
        ],
        in_specs=[pl.BlockSpec((devices, SUB, 3 * HD), lambda n: (0, last, 0))],
        out_specs=[
            pl.BlockSpec((span, devices, HD), lambda n: (0, 0, 0)),
            pl.BlockSpec((span, groups, wide), lambda n: (0, 0, 0)),
            pl.BlockSpec((1, 1), lambda n: (0, 0)),
        ],
        compiler_params=pltpu.CompilerParams(vmem_limit_bytes=VMEM_LIMIT),
        name="plan_rows",
    )(received)
    return offsets[:, :, 0].reshape(-1), places, crowded[0, 0] > 0


def attend_kernel(rows, span, win, block, shifts, apart, number_ref, place_ref, first_ref, *refs):
    out_refs = refs[-11 - (span if apart else 1) : -11]
    q_all, k_all, v_all, windows, begins, top, mixed, scores, weights, fades, totals = refs[-11:]
    groups, wide = place_ref.shape[1:]
    per = wide // win
    devices = groups * per
    units = devices // span
    blocks = span * rows // block
    lanes = [slice(n * HD, (n + 1) * HD) for n in range(block // HD)]

    def low_of(i):
        return number_ref[2 + i]

    def high_of(i):
        return number_ref[2 + blocks + i]

    part = min(64, block)

    @pl.when(high_of(blocks - 1) > 0)
    def _():
        for n in range(span * rows // HD):
            begin = jnp.broadcast_to(first_ref[n : n + 1, :], (HD, HD))
            begins[n * HD : (n + 1) * HD, :] = jnp.transpose(begin)

    spot = lax.broadcasted_iota(jnp.int32, (rows, wide), 0)
    for d in range(span):
        here = slice(d * rows, (d + 1) * rows)
        window = windows[d % 2]
        for n in range(devices):
            source = n
            if shifts:
                a, b = shifts[n]
                source = lax.rem(number_ref[1] + units - a, units) * span
                source += lax.rem(number_ref[0] + span - b, span)
            offset = pl.multiple_of(number_ref[2 + 2 * blocks + d * devices + source], SUB)
            piece = refs[n][pl.ds(offset, win), :] if shifts else refs[0][n, pl.ds(offset, win), :]
            slot = source % groups * wide + source // groups * win
            window[pl.ds(pl.multiple_of(slot, SUB), win), :] = piece
        onehot = [
            jnp.where(spot == place_ref[d, p : p + 1, :] - d * rows, 1.0, 0.0).astype(jnp.bfloat16)
            for p in range(groups)
        ]
        onehot = jnp.concatenate(onehot, axis=1) if groups > 1 else onehot[0]
        placed = jnp.dot(onehot, window[...], preferred_element_type=jnp.float32)
        scaled = placed[:, :HD] * EXP2_SCALE
        high = scaled.astype(jnp.bfloat16)
        q_all[here, :HD] = high
        q_all[here, HD:] = (scaled - high.astype(jnp.float32)).astype(jnp.bfloat16)
        key = placed[:, HD : 2 * HD].astype(jnp.bfloat16)
        k_all[here, :HD] = key
        k_all[here, HD:] = key
        v_all[here, :HD] = placed[:, 2 * HD :].astype(jnp.bfloat16)

    def starting(index):
        return pl.multiple_of(index * block, block)

    def score(i, j, slot):
        scores[slot][...] = lax.dot_general(
            q_all[pl.ds(starting(i), block), :],
            k_all[pl.ds(starting(j), block), :],
            (((1,), (1,)), ((), ())),
            preferred_element_type=jnp.float32,
        )

    def mix(j, slot):
        mixed[...] = mixed[...] * fades[slot][...] + jnp.dot(
            weights[slot][...], v_all[pl.ds(starting(j), block), :HD], preferred_element_type=jnp.float32
        )

    def weigh(i, j, fresh, slot, diagonal, bounded):
        lane = lax.broadcasted_iota(jnp.int32, (part, HD), 1)
        down = lax.broadcasted_iota(jnp.int32, (part, HD), 0)
        for r in range(0, block, part):
            here = slice(r, r + part)
            if bounded:
                begin = begins[pl.ds(pl.multiple_of(i * block + r, part), part), :] - starting(j) - lane
            columns = []
            for n, cols in enumerate(lanes):
                if diagonal and n * HD >= r + part:
                    break
                raw = scores[slot][here, cols]
                if bounded:
                    raw = jnp.where(begin <= n * HD, raw, NEG)
                if diagonal and (n + 1) * HD > r + 1:
                    raw = jnp.where(lane - down <= r - n * HD, raw, NEG)
                columns.append(raw)
            peak = functools.reduce(jnp.maximum, columns)
            old = jnp.where(fresh, NEG, top[here, :])
            new = jnp.maximum(old, jnp.max(peak, axis=1, keepdims=True))
            fade = jnp.exp2(old - new)
            total = totals[1 - slot][here, :] * fade
            for n, cols in enumerate(lanes):
                if n < len(columns):
                    weight = jnp.exp2(columns[n] - new)
                    total += weight
                    weights[slot][here, cols] = weight.astype(jnp.bfloat16)
                else:
                    weights[slot][here, cols] = jnp.zeros((part, HD), jnp.bfloat16)
            top[here, :] = new
            fades[slot][here, :] = fade
            totals[slot][here, :] = total

    def finish(i, slot):
        total = jnp.sum(totals[slot][...], axis=1, keepdims=True)
        v_all[pl.ds(starting(i), block), HD:] = (mixed[...] / total).astype(jnp.bfloat16)

    def step(state, slot):
        last_i, last_j, i, j = state
        done = j == i
        next_i = jnp.where(done, jnp.minimum(i + 1, blocks - 1), i)
        next_j = jnp.where(done, low_of(next_i), j + 1)
        bounded = high_of(i) > j * block
        fresh = j == low_of(i)

        def work(diagonal, bounded):
            mix(last_j, 1 - slot)
            score(next_i, next_j, 1 - slot)
            weigh(i, j, fresh, slot, diagonal, bounded)

        @pl.when(done & bounded)
        def _():
            work(True, True)

        @pl.when(done & jnp.logical_not(bounded))
        def _():
            work(True, False)

        @pl.when(jnp.logical_not(done) & bounded)
        def _():
            work(False, True)

        @pl.when(jnp.logical_not(done | bounded))
        def _():
            work(False, False)

        @pl.when(last_j == last_i)
        def _():
            finish(last_i, 1 - slot)

        return i, j, next_i, next_j

    pairs = blocks * (blocks + 1) // 2
    for i in range(blocks):
        pairs -= low_of(i)
    mixed[...] = jnp.zeros_like(mixed)
    for slot in range(2):
        weights[slot][...] = jnp.zeros_like(weights[slot])
        fades[slot][...] = jnp.zeros_like(fades[slot])
        totals[slot][...] = jnp.zeros_like(totals[slot])
    top[...] = jnp.full_like(top, NEG)
    score(0, 0, 0)

    def two_steps(n, state):
        middle = step(state, 0)
        after = step_if(2 * n + 1 < pairs, middle)
        return after

    def step_if(more, state):
        _, _, i, j = state
        done = j == i
        next_i = jnp.where(done, jnp.minimum(i + 1, blocks - 1), i)
        next_j = jnp.where(done, low_of(next_i), j + 1)

        @pl.when(more)
        def _():
            step(state, 1)

        return i, j, next_i, next_j

    zero = jnp.int32(0)
    lax.fori_loop(0, (pairs + 1) // 2, two_steps, (zero + 1, zero, zero, zero))

    for slot in range(2):

        @pl.when(pairs % 2 == 1 - slot)
        def _():
            mix(blocks - 1, slot)
            finish(blocks - 1, slot)

    for k in range(span):
        if len(out_refs) == 1:
            out_refs[0][k] = v_all[k * rows : (k + 1) * rows, HD:]
        else:
            owner = lax.rem(number_ref[0] + k, span)
            out_refs[k][...] = v_all[pl.ds(pl.multiple_of(owner * rows, SUB), rows), HD:]


def attend(received, shifts, apart, after, numbers, places, first, rows, span, win, block):
    total = received[0].shape[-2]
    devices = sum(piece.size for piece in received) // (total * 3 * HD)
    length = span * rows
    vmem = pl.BlockSpec(memory_space=pltpu.VMEM)
    smem = pl.BlockSpec(memory_space=pltpu.SMEM)
    narrow = pltpu.VMEM((block, HD), jnp.float32)
    return pl.pallas_call(
        functools.partial(attend_kernel, rows, span, win, block, shifts, apart),
        out_shape=[jax.ShapeDtypeStruct((rows, HD), jnp.bfloat16)] * span
        if apart
        else [jax.ShapeDtypeStruct((span, rows, HD), jnp.bfloat16)],
        in_specs=[smem] + [vmem] * (2 + len(received)) + [pl.BlockSpec(memory_space=pl.ANY)] * len(after),
        out_specs=[vmem] * (span if apart else 1),
        scratch_shapes=[
            pltpu.VMEM((length, 2 * HD), jnp.bfloat16),
            pltpu.VMEM((length, 2 * HD), jnp.bfloat16),
            pltpu.VMEM((length, 2 * HD), jnp.bfloat16),
            [pltpu.VMEM((devices * win, 3 * HD), jnp.bfloat16)] * 2,
            pltpu.VMEM((length, HD), jnp.int32),
            narrow,
            narrow,
            [pltpu.VMEM((block, block), jnp.float32)] * 2,
            [pltpu.VMEM((block, block), jnp.bfloat16)] * 2,
            [narrow] * 2,
            [narrow] * 2,
        ],
        compiler_params=pltpu.CompilerParams(vmem_limit_bytes=VMEM_LIMIT),
        cost_estimate=pl.CostEstimate(
            flops=2 * length * devices * win * 3 * HD + 8 * length * length * HD,
            bytes_accessed=2 * (devices * total * 3 * HD + length * HD),
            transcendentals=length * length // 2,
        ),
        name="attend_head",
    )(numbers, places, first.reshape(length // HD, HD), *received, *after)


def join_kernel(span, own_ref, *refs):
    out_ref = refs[-1]
    n = 0
    for ref in refs[:-1]:
        for m in range(ref.shape[0] if len(ref.shape) == 3 else 1):
            if len(ref.shape) == 3:
                out_ref[:, n * HD : (n + 1) * HD] = ref[m]
            else:
                head = n // span * span + lax.rem(own_ref[0] + span - n % span, span)
                out_ref[:, pl.ds(pl.multiple_of(head * HD, HD), HD)] = ref[...]
            n += 1


def join_heads(own, pieces, span):
    vmem = pl.BlockSpec(memory_space=pltpu.VMEM)
    smem = pl.BlockSpec(memory_space=pltpu.SMEM)
    rows = pieces[0].shape[-2]
    width = sum(piece.size for piece in pieces) // rows
    return pl.pallas_call(
        functools.partial(join_kernel, span),
        out_shape=jax.ShapeDtypeStruct((rows, width), jnp.bfloat16),
        in_specs=[smem] + [vmem] * len(pieces),
        out_specs=vmem,
        compiler_params=pltpu.CompilerParams(vmem_limit_bytes=VMEM_LIMIT),
        name="join_heads",
    )(own, *pieces)


def body(queries, keys, values, target_row, doc_lengths):
    rows, width = queries.shape
    group = width // HD
    devices = lax.axis_size("seq")
    span = max(group // 2, 1)
    units = devices // span
    each = group // span
    length = span * rows
    pair_most = 3 * rows // (2 * devices)
    mean = rows // units
    most = min(pair_most * span, rows)
    usual = min(mean + mean // 16, most)
    index = lax.axis_index("seq")
    own = jnp.stack([index % span, index // span]).astype(jnp.int32)
    unit_start = index // span * length

    docs = jnp.arange(doc_lengths.shape[0])
    starts = jnp.sum(jnp.where(docs[:, None] < docs[None, :], doc_lengths[:, None], 0), axis=0)
    positions = unit_start + jnp.arange(length, dtype=jnp.int32)
    first = jnp.max(jnp.where(starts[None, :] <= positions[:, None], starts[None, :], 0), axis=1)
    first = jnp.maximum(first - unit_start, 0)
    block = math.gcd(length, 512)
    settings = jnp.concatenate([own, first[::block] // block, first[block - 1 :: block]])

    def moved(piece, a, b):
        if a == 0 and b == 0:
            return piece
        route = [
            (u * span + m, (u + a) % units * span + (m + b) % span)
            for u in range(units)
            for m in range(span)
        ]
        return lax.ppermute(piece, "seq", route)

    members = [[u * span + m for m in range(span)] for u in range(units)]
    shifts = tuple((a, b) for a in range(units) for b in range(span))

    def attended(cap):
        total = rounded_up(cap + 3, SUB)
        win = SUB
        while win < pair_most + SUB - 1:
            win *= 2
        win = min(total, win)
        arrived = []
        for chunk in range(each):
            if chunk == 0:
                sent = sort_rows(queries, keys, values, target_row, units, span, cap, total, chunk)
                arrived.append([lax.all_to_all(sent, "seq", split_axis=0, concat_axis=0, tiled=True)])
            else:
                sent = sort_apart(
                    queries, keys, values, target_row, own, units, span, cap, total, chunk, shifts
                )
                arrived.append([moved(piece, a, b) for piece, (a, b) in zip(sent, shifts)])
        offsets, places, crowded = plan_rows(arrived[0][0], devices, span, rows, total, win)
        numbers = jnp.concatenate([settings, offsets])
        pieces = []
        after = arrived[1][1:-QUEUED] if each > 1 else []
        for chunk in range(each):
            apart = chunk == each - 1
            heads = attend(
                arrived[chunk], shifts if chunk else (), apart, after, numbers, places, first, rows, span, win, block
            )
            after = heads
            if apart:
                pieces += [moved(heads[b], 0, b) for b in range(span)]
            else:
                pieces.append(
                    lax.all_to_all(
                        heads[0], "seq", split_axis=0, concat_axis=0, tiled=True, axis_index_groups=members
                    )
                )
        return pieces, crowded

    pieces, crowded = attended(usual)
    if usual == most:
        return join_heads(own, pieces, span)
    return lax.cond(
        crowded,
        lambda: join_heads(own, attended(most)[0], span),
        lambda: join_heads(own, pieces, span),
    )


def solution(mesh):
    in_specs = (P("seq", "head"), P("seq", "head"), P("seq", "head"), P("seq"), P())
    out_specs = P("seq", "head")
    return jax.shard_map(body, mesh=mesh, in_specs=in_specs, out_specs=out_specs, check_vma=False)
```

```python
import functools
import math

import jax
import jax.numpy as jnp
from jax import lax
from jax.experimental import pallas as pl
from jax.experimental.pallas import tpu as pltpu
from jax.sharding import PartitionSpec as P

HD = 128
SUB = 16
BASE = 64
NEG = -1e30
EXP2_SCALE = math.log2(math.e) / math.sqrt(HD)
VMEM_LIMIT = 40 * 1024 * 1024
LARGE_LIMIT = 60 * 1024 * 1024


def rounded_up(count, multiple):
    return -(-count // multiple) * multiple


def sort_kernel(units, span_rows, cap, total, target_ref, q_ref, k_ref, v_ref, out_ref, onehot, notes):
    rows = q_ref.shape[0]
    lanes = 3 * HD

    @pl.when(pl.program_id(0) == 0)
    def _():
        across = jnp.concatenate([target_ref[n : n + 1, :] for n in range(rows // HD)], axis=1)
        down = jnp.concatenate(
            [
                jnp.transpose(jnp.broadcast_to(target_ref[n : n + 1, :], (HD, HD)))
                for n in range(rows // HD)
            ],
            axis=0,
        )
        down = jnp.concatenate([down] * (rows // HD), axis=1)
        unit = jnp.zeros_like(across)
        for u in range(1, units):
            unit += (across >= u * span_rows).astype(jnp.int32)
        inner = across - unit * span_rows
        before = (down < across) & (down >= unit * span_rows)
        place = jnp.sum(before.astype(jnp.int32), axis=0, keepdims=True)
        slot = jnp.where(place < cap, unit * total + place, -1)
        slots = lax.broadcasted_iota(jnp.int32, (units * total, rows), 0)
        onehot[...] = jnp.where(slots == slot, 1.0, 0.0).astype(jnp.bfloat16)
        crowded = jnp.max(jnp.where(place >= cap, 1.0, 0.0), axis=1, keepdims=True)
        high = inner // BASE
        kind = lax.broadcasted_iota(jnp.int32, (SUB, rows), 0)
        digits = jnp.where(kind == 0, high + 1, jnp.where(kind == 1, inner - high * BASE, 0))
        digits = digits.astype(jnp.float32).astype(jnp.bfloat16)
        spread = lax.broadcasted_iota(jnp.int32, (lanes, rows), 0)
        line = lax.broadcasted_iota(jnp.int32, (total, lanes), 0)
        for u in range(units):
            mine = jnp.where((spread == place) & (unit == u), 1.0, 0.0).astype(jnp.bfloat16)
            along = lax.dot_general(
                digits, mine, (((1,), (1,)), ((), ())), preferred_element_type=jnp.float32
            )
            note = jnp.where(line == total - 3, along[0:1], jnp.where(line == total - 2, along[1:2], 0.0))
            note = jnp.where(line == total - 1, crowded, note)
            notes[u * total : (u + 1) * total, :] = note.astype(jnp.bfloat16)

    for m in range(q_ref.shape[1] // HD):
        cols = slice(m * HD, (m + 1) * HD)
        block = jnp.concatenate([q_ref[:, cols], k_ref[:, cols], v_ref[:, cols]], axis=1)
        sent = jnp.dot(onehot[...], block, preferred_element_type=jnp.float32).astype(jnp.bfloat16)
        out_ref[:, m] = (sent + notes[...]).reshape(units, total, lanes)


def sort_rows(queries, keys, values, target_row, units, span, cap, total, chunk):
    rows = queries.shape[0]
    steps = math.gcd(span, 4)
    count = span // steps
    column = pl.BlockSpec((rows, count * HD), lambda n: (0, chunk * steps + n))
    sent = pl.pallas_call(
        functools.partial(sort_kernel, units, span * rows, cap, total),
        grid=(steps,),
        out_shape=jax.ShapeDtypeStruct((units, span, total, 3 * HD), jnp.bfloat16),
        in_specs=[
            pl.BlockSpec((rows // HD, HD), lambda n: (0, 0)),
            column,
            column,
            column,
        ],
        out_specs=pl.BlockSpec((units, count, total, 3 * HD), lambda n: (0, n, 0, 0)),
        scratch_shapes=[
            pltpu.VMEM((units * total, rows), jnp.bfloat16),
            pltpu.VMEM((units * total, 3 * HD), jnp.bfloat16),
        ],
        compiler_params=pltpu.CompilerParams(vmem_limit_bytes=LARGE_LIMIT),
        cost_estimate=pl.CostEstimate(
            flops=2 * units * span * total * rows * 3 * HD,
            bytes_accessed=2 * 3 * HD * span * (rows + units * total),
            transcendentals=0,
        ),
        name="sort_rows",
    )(target_row.reshape(rows // HD, HD), queries, keys, values)
    return sent.reshape(units * span, total, 3 * HD)


def plan_kernel(devices, span, rows, total, win, *refs):
    tail_ref, offset_ref, place_ref, crowded_ref = refs
    tail = tail_ref[...].astype(jnp.float32)
    lines = [tail[n, SUB - 3 :, :] for n in range(devices)]
    high = jnp.concatenate([line[0:1] for line in lines], axis=0)
    low = jnp.concatenate([line[1:2] for line in lines], axis=0)
    crowded = jnp.concatenate([line[2:3] for line in lines], axis=0)
    crowded_ref[...] = jnp.max(jnp.max(crowded, axis=1, keepdims=True), axis=0, keepdims=True).astype(jnp.int32)
    place = jnp.where(high > 0.0, (high - 1.0) * BASE + low, -1.0).astype(jnp.int32)
    per = max(HD // win, 1)
    groups = devices // per
    wide = per * win
    lane = lax.broadcasted_iota(jnp.int32, (groups, wide), 1)
    shifted = {}
    for t in range((total - win) // SUB + 1):
        for e in range(per):
            turn = (e * win - SUB * t) % (3 * HD)
            part = place[e * groups : (e + 1) * groups]
            shifted[t, e] = (pltpu.roll(part, turn, 1) if turn else part)[:, :wide]
    for d in range(span):
        begun = jnp.sum(jnp.where((place >= 0) & (place < d * rows), 1, 0), axis=1, keepdims=True)
        offset = jnp.minimum(begun // SUB * SUB, total - win)
        offset_ref[d] = jnp.broadcast_to(offset, (devices, HD))
        out = jnp.full((groups, wide), -1, jnp.int32)
        for (t, e), part in shifted.items():
            mine = (offset[e * groups : (e + 1) * groups] == SUB * t) & (lane >= e * win) & (lane < (e + 1) * win)
            out = jnp.where(mine, part, out)
        place_ref[d] = out


def plan_rows(received, devices, span, rows, total, win):
    wide = max(HD // win, 1) * win
    groups = devices * win // wide
    last = total // SUB - 1
    offsets, places, crowded = pl.pallas_call(
        functools.partial(plan_kernel, devices, span, rows, total, win),
        grid=(1,),
        out_shape=[
            jax.ShapeDtypeStruct((span, devices, HD), jnp.int32),
            jax.ShapeDtypeStruct((span, groups, wide), jnp.int32),
            jax.ShapeDtypeStruct((1, 1), jnp.int32),
        ],
        in_specs=[pl.BlockSpec((devices, SUB, 3 * HD), lambda n: (0, last, 0))],
        out_specs=[
            pl.BlockSpec((span, devices, HD), lambda n: (0, 0, 0)),
            pl.BlockSpec((span, groups, wide), lambda n: (0, 0, 0)),
            pl.BlockSpec((1, 1), lambda n: (0, 0)),
        ],
        compiler_params=pltpu.CompilerParams(vmem_limit_bytes=VMEM_LIMIT),
        name="plan_rows",
    )(received)
    return offsets[:, :, 0].reshape(-1), places, crowded[0, 0] > 0


def attend_kernel(rows, span, win, block, number_ref, place_ref, first_ref, recv_ref, *refs):
    out_refs = refs[-11 - span : -11]
    q_all, k_all, v_all, windows, begins, top, mixed, scores, weights, fades, totals = refs[-11:]
    devices = recv_ref.shape[0]
    groups, wide = place_ref.shape[1:]
    per = wide // win
    blocks = span * rows // block
    lanes = [slice(n * HD, (n + 1) * HD) for n in range(block // HD)]

    def low_of(i):
        return number_ref[1 + i]

    def high_of(i):
        return number_ref[1 + blocks + i]

    part = min(64, block)

    @pl.when(high_of(blocks - 1) > 0)
    def _():
        for n in range(span * rows // HD):
            begin = jnp.broadcast_to(first_ref[n : n + 1, :], (HD, HD))
            begins[n * HD : (n + 1) * HD, :] = jnp.transpose(begin)

    spot = lax.broadcasted_iota(jnp.int32, (rows, wide), 0)
    for d in range(span):
        here = slice(d * rows, (d + 1) * rows)
        window = windows[d % 2]
        for p in range(groups):
            for e in range(per):
                i = e * groups + p
                offset = pl.multiple_of(number_ref[1 + 2 * blocks + d * devices + i], SUB)
                slot = p * wide + e * win
                window[slot : slot + win, :] = recv_ref[i, pl.ds(offset, win), :]
        onehot = [
            jnp.where(spot == place_ref[d, p : p + 1, :] - d * rows, 1.0, 0.0).astype(jnp.bfloat16)
            for p in range(groups)
        ]
        onehot = jnp.concatenate(onehot, axis=1) if groups > 1 else onehot[0]
        placed = jnp.dot(onehot, window[...], preferred_element_type=jnp.float32)
        scaled = placed[:, :HD] * EXP2_SCALE
        high = scaled.astype(jnp.bfloat16)
        q_all[here, :HD] = high
        q_all[here, HD:] = (scaled - high.astype(jnp.float32)).astype(jnp.bfloat16)
        key = placed[:, HD : 2 * HD].astype(jnp.bfloat16)
        k_all[here, :HD] = key
        k_all[here, HD:] = key
        v_all[here, :HD] = placed[:, 2 * HD :].astype(jnp.bfloat16)

    def starting(index):
        return pl.multiple_of(index * block, block)

    def score(i, j, slot):
        scores[slot][...] = lax.dot_general(
            q_all[pl.ds(starting(i), block), :],
            k_all[pl.ds(starting(j), block), :],
            (((1,), (1,)), ((), ())),
            preferred_element_type=jnp.float32,
        )

    def mix(j, slot):
        mixed[...] = mixed[...] * fades[slot][...] + jnp.dot(
            weights[slot][...], v_all[pl.ds(starting(j), block), :HD], preferred_element_type=jnp.float32
        )

    def weigh(i, j, fresh, slot, diagonal, bounded):
        lane = lax.broadcasted_iota(jnp.int32, (part, HD), 1)
        down = lax.broadcasted_iota(jnp.int32, (part, HD), 0)
        for r in range(0, block, part):
            here = slice(r, r + part)
            if bounded:
                begin = begins[pl.ds(pl.multiple_of(i * block + r, part), part), :] - starting(j) - lane
            columns = []
            for n, cols in enumerate(lanes):
                if diagonal and n * HD >= r + part:
                    break
                raw = scores[slot][here, cols]
                if bounded:
                    raw = jnp.where(begin <= n * HD, raw, NEG)
                if diagonal and (n + 1) * HD > r + 1:
                    raw = jnp.where(lane - down <= r - n * HD, raw, NEG)
                columns.append(raw)
            peak = functools.reduce(jnp.maximum, columns)
            old = jnp.where(fresh, NEG, top[here, :])
            new = jnp.maximum(old, jnp.max(peak, axis=1, keepdims=True))
            fade = jnp.exp2(old - new)
            total = totals[1 - slot][here, :] * fade
            for n, cols in enumerate(lanes):
                if n < len(columns):
                    weight = jnp.exp2(columns[n] - new)
                    total += weight
                    weights[slot][here, cols] = weight.astype(jnp.bfloat16)
                else:
                    weights[slot][here, cols] = jnp.zeros((part, HD), jnp.bfloat16)
            top[here, :] = new
            fades[slot][here, :] = fade
            totals[slot][here, :] = total

    def finish(i, slot):
        total = jnp.sum(totals[slot][...], axis=1, keepdims=True)
        v_all[pl.ds(starting(i), block), HD:] = (mixed[...] / total).astype(jnp.bfloat16)

    def step(state, slot):
        last_i, last_j, i, j = state
        done = j == i
        next_i = jnp.where(done, jnp.minimum(i + 1, blocks - 1), i)
        next_j = jnp.where(done, low_of(next_i), j + 1)
        bounded = high_of(i) > j * block
        fresh = j == low_of(i)

        def work(diagonal, bounded):
            mix(last_j, 1 - slot)
            score(next_i, next_j, 1 - slot)
            weigh(i, j, fresh, slot, diagonal, bounded)

        @pl.when(done & bounded)
        def _():
            work(True, True)

        @pl.when(done & jnp.logical_not(bounded))
        def _():
            work(True, False)

        @pl.when(jnp.logical_not(done) & bounded)
        def _():
            work(False, True)

        @pl.when(jnp.logical_not(done | bounded))
        def _():
            work(False, False)

        @pl.when(last_j == last_i)
        def _():
            finish(last_i, 1 - slot)

        return i, j, next_i, next_j

    pairs = blocks * (blocks + 1) // 2
    for i in range(blocks):
        pairs -= low_of(i)
    mixed[...] = jnp.zeros_like(mixed)
    for slot in range(2):
        weights[slot][...] = jnp.zeros_like(weights[slot])
        fades[slot][...] = jnp.zeros_like(fades[slot])
        totals[slot][...] = jnp.zeros_like(totals[slot])
    top[...] = jnp.full_like(top, NEG)
    score(0, 0, 0)

    def two_steps(n, state):
        middle = step(state, 0)
        after = step_if(2 * n + 1 < pairs, middle)
        return after

    def step_if(more, state):
        _, _, i, j = state
        done = j == i
        next_i = jnp.where(done, jnp.minimum(i + 1, blocks - 1), i)
        next_j = jnp.where(done, low_of(next_i), j + 1)

        @pl.when(more)
        def _():
            step(state, 1)

        return i, j, next_i, next_j

    zero = jnp.int32(0)
    lax.fori_loop(0, (pairs + 1) // 2, two_steps, (zero + 1, zero, zero, zero))

    for slot in range(2):

        @pl.when(pairs % 2 == 1 - slot)
        def _():
            mix(blocks - 1, slot)
            finish(blocks - 1, slot)

    for k in range(span):
        owner = lax.rem(number_ref[0] + k, span)
        out_refs[k][...] = v_all[pl.ds(pl.multiple_of(owner * rows, SUB), rows), HD:]


def attend(received, after, numbers, places, first, rows, span, win, block, limit):
    devices, total, _ = received.shape
    length = span * rows
    vmem = pl.BlockSpec(memory_space=pltpu.VMEM)
    smem = pl.BlockSpec(memory_space=pltpu.SMEM)
    narrow = pltpu.VMEM((block, HD), jnp.float32)
    return pl.pallas_call(
        functools.partial(attend_kernel, rows, span, win, block),
        out_shape=[jax.ShapeDtypeStruct((rows, HD), jnp.bfloat16)] * span,
        in_specs=[smem] + [vmem] * 3 + [pl.BlockSpec(memory_space=pl.ANY)] * len(after),
        out_specs=[vmem] * span,
        scratch_shapes=[
            pltpu.VMEM((length, 2 * HD), jnp.bfloat16),
            pltpu.VMEM((length, 2 * HD), jnp.bfloat16),
            pltpu.VMEM((length, 2 * HD), jnp.bfloat16),
            [pltpu.VMEM((devices * win, 3 * HD), jnp.bfloat16)] * 2,
            pltpu.VMEM((length, HD), jnp.int32),
            narrow,
            narrow,
            [pltpu.VMEM((block, block), jnp.float32)] * 2,
            [pltpu.VMEM((block, block), jnp.bfloat16)] * 2,
            [narrow] * 2,
            [narrow] * 2,
        ],
        compiler_params=pltpu.CompilerParams(vmem_limit_bytes=limit),
        cost_estimate=pl.CostEstimate(
            flops=2 * length * devices * win * 3 * HD + 8 * length * length * HD,
            bytes_accessed=2 * (devices * total * 3 * HD + length * HD),
            transcendentals=length * length // 2,
        ),
        name="attend_head",
    )(numbers, places, first.reshape(length // HD, HD), received, *after)


def join_kernel(span, own_ref, *refs):
    out_ref = refs[-1]
    for n, ref in enumerate(refs[:-1]):
        head = n // span * span + lax.rem(own_ref[0] + span - n % span, span)
        out_ref[:, pl.ds(pl.multiple_of(head * HD, HD), HD)] = ref[...]


def join_heads(own, pieces, span):
    vmem = pl.BlockSpec(memory_space=pltpu.VMEM)
    smem = pl.BlockSpec(memory_space=pltpu.SMEM)
    rows = pieces[0].shape[0]
    return pl.pallas_call(
        functools.partial(join_kernel, span),
        out_shape=jax.ShapeDtypeStruct((rows, len(pieces) * HD), jnp.bfloat16),
        in_specs=[smem] + [vmem] * len(pieces),
        out_specs=vmem,
        compiler_params=pltpu.CompilerParams(vmem_limit_bytes=VMEM_LIMIT),
        name="join_heads",
    )(own, *pieces)


def body(queries, keys, values, target_row, doc_lengths):
    rows, width = queries.shape
    group = width // HD
    devices = lax.axis_size("seq")
    span = max(group // 2, 1)
    units = devices // span
    each = group // span
    length = span * rows
    pair_most = 3 * rows // (2 * devices)
    mean = rows // units
    most = min(pair_most * span, rows)
    usual = min(mean + mean // 16, most)
    index = lax.axis_index("seq")
    own = (index % span).astype(jnp.int32).reshape(1)
    unit_start = index // span * length

    docs = jnp.arange(doc_lengths.shape[0])
    starts = jnp.sum(jnp.where(docs[:, None] < docs[None, :], doc_lengths[:, None], 0), axis=0)
    positions = unit_start + jnp.arange(length, dtype=jnp.int32)
    first = jnp.max(jnp.where(starts[None, :] <= positions[:, None], starts[None, :], 0), axis=1)
    first = jnp.maximum(first - unit_start, 0)
    block = math.gcd(length, 512)
    settings = jnp.concatenate([own, first[::block] // block, first[block - 1 :: block]])

    def homeward(piece, shift):
        if shift == 0:
            return piece
        route = [
            (u * span + m, u * span + (m + shift) % span) for u in range(units) for m in range(span)
        ]
        return lax.ppermute(piece, "seq", route)

    def attended(cap):
        total = rounded_up(cap + 3, SUB)
        win = SUB
        while win < pair_most + SUB - 1:
            win *= 2
        win = min(total, win)
        pieces = []
        after = []
        for chunk in range(each):
            sent = sort_rows(queries, keys, values, target_row, units, span, cap, total, chunk)
            received = lax.all_to_all(sent, "seq", split_axis=0, concat_axis=0, tiled=True)
            if chunk == 0:
                offsets, places, crowded = plan_rows(received, devices, span, rows, total, win)
                numbers = jnp.concatenate([settings, offsets])
            limit = LARGE_LIMIT if chunk == 0 else VMEM_LIMIT
            heads = attend(received, after, numbers, places, first, rows, span, win, block, limit)
            far_first = sorted(range(span), key=lambda shift: -min(shift, span - shift))
            sent = {shift: homeward(heads[shift], shift) for shift in far_first}
            after = [sent[shift] for shift in range(span)]
            pieces += after
        return pieces, crowded

    pieces, crowded = attended(usual)
    if usual == most:
        return join_heads(own, pieces, span)
    return lax.cond(
        crowded,
        lambda: join_heads(own, attended(most)[0], span),
        lambda: join_heads(own, pieces, span),
    )


def solution(mesh):
    in_specs = (P("seq", "head"), P("seq", "head"), P("seq", "head"), P("seq"), P())
    out_specs = P("seq", "head")
    return jax.shard_map(body, mesh=mesh, in_specs=in_specs, out_specs=out_specs, check_vma=False)
```

```python
import functools
import math

import jax
import jax.numpy as jnp
from jax import lax
from jax.experimental import pallas as pl
from jax.experimental.pallas import tpu as pltpu
from jax.sharding import PartitionSpec as P

HD = 128
SUB = 16
BASE = 64
NEG = -1e30
EXP2_SCALE = math.log2(math.e) / math.sqrt(HD)
VMEM_LIMIT = 40 * 1024 * 1024
SORT_LIMIT = 60 * 1024 * 1024


def rounded_up(count, multiple):
    return -(-count // multiple) * multiple


def sort_kernel(units, span_rows, cap, total, target_ref, q_ref, k_ref, v_ref, out_ref, onehot, notes):
    rows = q_ref.shape[0]
    lanes = 3 * HD

    @pl.when(pl.program_id(0) == 0)
    def _():
        across = jnp.concatenate([target_ref[n : n + 1, :] for n in range(rows // HD)], axis=1)
        down = jnp.concatenate(
            [
                jnp.transpose(jnp.broadcast_to(target_ref[n : n + 1, :], (HD, HD)))
                for n in range(rows // HD)
            ],
            axis=0,
        )
        down = jnp.concatenate([down] * (rows // HD), axis=1)
        unit = jnp.zeros_like(across)
        for u in range(1, units):
            unit += (across >= u * span_rows).astype(jnp.int32)
        inner = across - unit * span_rows
        before = (down < across) & (down >= unit * span_rows)
        place = jnp.sum(before.astype(jnp.int32), axis=0, keepdims=True)
        slot = jnp.where(place < cap, unit * total + place, -1)
        slots = lax.broadcasted_iota(jnp.int32, (units * total, rows), 0)
        onehot[...] = jnp.where(slots == slot, 1.0, 0.0).astype(jnp.bfloat16)
        crowded = jnp.max(jnp.where(place >= cap, 1.0, 0.0), axis=1, keepdims=True)
        high = inner // BASE
        kind = lax.broadcasted_iota(jnp.int32, (SUB, rows), 0)
        digits = jnp.where(kind == 0, high + 1, jnp.where(kind == 1, inner - high * BASE, 0))
        digits = digits.astype(jnp.float32).astype(jnp.bfloat16)
        spread = lax.broadcasted_iota(jnp.int32, (lanes, rows), 0)
        line = lax.broadcasted_iota(jnp.int32, (total, lanes), 0)
        for u in range(units):
            mine = jnp.where((spread == place) & (unit == u), 1.0, 0.0).astype(jnp.bfloat16)
            along = lax.dot_general(
                digits, mine, (((1,), (1,)), ((), ())), preferred_element_type=jnp.float32
            )
            note = jnp.where(line == total - 3, along[0:1], jnp.where(line == total - 2, along[1:2], 0.0))
            note = jnp.where(line == total - 1, crowded, note)
            notes[u * total : (u + 1) * total, :] = note.astype(jnp.bfloat16)

    for m in range(q_ref.shape[1] // HD):
        cols = slice(m * HD, (m + 1) * HD)
        block = jnp.concatenate([q_ref[:, cols], k_ref[:, cols], v_ref[:, cols]], axis=1)
        sent = jnp.dot(onehot[...], block, preferred_element_type=jnp.float32).astype(jnp.bfloat16)
        out_ref[:, m] = (sent + notes[...]).reshape(units, total, lanes)


def sort_rows(queries, keys, values, target_row, units, span, cap, total, chunk):
    rows = queries.shape[0]
    steps = math.gcd(span, 2)
    count = span // steps
    column = pl.BlockSpec((rows, count * HD), lambda n: (0, chunk * steps + n))
    sent = pl.pallas_call(
        functools.partial(sort_kernel, units, span * rows, cap, total),
        grid=(steps,),
        out_shape=jax.ShapeDtypeStruct((units, span, total, 3 * HD), jnp.bfloat16),
        in_specs=[
            pl.BlockSpec((rows // HD, HD), lambda n: (0, 0)),
            column,
            column,
            column,
        ],
        out_specs=pl.BlockSpec((units, count, total, 3 * HD), lambda n: (0, n, 0, 0)),
        scratch_shapes=[
            pltpu.VMEM((units * total, rows), jnp.bfloat16),
            pltpu.VMEM((units * total, 3 * HD), jnp.bfloat16),
        ],
        compiler_params=pltpu.CompilerParams(vmem_limit_bytes=SORT_LIMIT),
        cost_estimate=pl.CostEstimate(
            flops=2 * units * span * total * rows * 3 * HD,
            bytes_accessed=2 * 3 * HD * span * (rows + units * total),
            transcendentals=0,
        ),
        name="sort_rows",
    )(target_row.reshape(rows // HD, HD), queries, keys, values)
    return sent.reshape(units * span, total, 3 * HD)


def plan_kernel(devices, span, rows, total, win, *refs):
    tail_ref, offset_ref, place_ref, crowded_ref = refs
    tail = tail_ref[...].astype(jnp.float32)
    lines = [tail[n, SUB - 3 :, :] for n in range(devices)]
    high = jnp.concatenate([line[0:1] for line in lines], axis=0)
    low = jnp.concatenate([line[1:2] for line in lines], axis=0)
    crowded = jnp.concatenate([line[2:3] for line in lines], axis=0)
    crowded_ref[...] = jnp.max(jnp.max(crowded, axis=1, keepdims=True), axis=0, keepdims=True).astype(jnp.int32)
    place = jnp.where(high > 0.0, (high - 1.0) * BASE + low, -1.0).astype(jnp.int32)
    per = max(HD // win, 1)
    groups = devices // per
    wide = per * win
    lane = lax.broadcasted_iota(jnp.int32, (groups, wide), 1)
    shifted = {}
    for t in range((total - win) // SUB + 1):
        for e in range(per):
            turn = (e * win - SUB * t) % (3 * HD)
            part = place[e * groups : (e + 1) * groups]
            shifted[t, e] = (pltpu.roll(part, turn, 1) if turn else part)[:, :wide]
    for d in range(span):
        begun = jnp.sum(jnp.where((place >= 0) & (place < d * rows), 1, 0), axis=1, keepdims=True)
        offset = jnp.minimum(begun // SUB * SUB, total - win)
        offset_ref[d] = jnp.broadcast_to(offset, (devices, HD))
        out = jnp.full((groups, wide), -1, jnp.int32)
        for (t, e), part in shifted.items():
            mine = (offset[e * groups : (e + 1) * groups] == SUB * t) & (lane >= e * win) & (lane < (e + 1) * win)
            out = jnp.where(mine, part, out)
        place_ref[d] = out


def plan_rows(received, devices, span, rows, total, win):
    wide = max(HD // win, 1) * win
    groups = devices * win // wide
    last = total // SUB - 1
    offsets, places, crowded = pl.pallas_call(
        functools.partial(plan_kernel, devices, span, rows, total, win),
        grid=(1,),
        out_shape=[
            jax.ShapeDtypeStruct((span, devices, HD), jnp.int32),
            jax.ShapeDtypeStruct((span, groups, wide), jnp.int32),
            jax.ShapeDtypeStruct((1, 1), jnp.int32),
        ],
        in_specs=[pl.BlockSpec((devices, SUB, 3 * HD), lambda n: (0, last, 0))],
        out_specs=[
            pl.BlockSpec((span, devices, HD), lambda n: (0, 0, 0)),
            pl.BlockSpec((span, groups, wide), lambda n: (0, 0, 0)),
            pl.BlockSpec((1, 1), lambda n: (0, 0)),
        ],
        compiler_params=pltpu.CompilerParams(vmem_limit_bytes=VMEM_LIMIT),
        name="plan_rows",
    )(received)
    return offsets[:, :, 0].reshape(-1), places, crowded[0, 0] > 0


def attend_kernel(rows, span, win, block, number_ref, place_ref, first_ref, recv_ref, *refs):
    out_refs = refs[-11 - span : -11]
    q_all, k_all, v_all, windows, begins, top, mixed, scores, weights, fades, totals = refs[-11:]
    devices = recv_ref.shape[0]
    groups, wide = place_ref.shape[1:]
    per = wide // win
    blocks = span * rows // block
    lanes = [slice(n * HD, (n + 1) * HD) for n in range(block // HD)]

    def low_of(i):
        return number_ref[1 + i]

    def high_of(i):
        return number_ref[1 + blocks + i]

    part = min(32, block)

    @pl.when(high_of(blocks - 1) > 0)
    def _():
        for n in range(span * rows // HD):
            begin = jnp.broadcast_to(first_ref[n : n + 1, :], (HD, HD))
            begins[n * HD : (n + 1) * HD, :] = jnp.transpose(begin)

    spot = lax.broadcasted_iota(jnp.int32, (rows, wide), 0)
    for d in range(span):
        here = slice(d * rows, (d + 1) * rows)
        window = windows[d % 2]
        for p in range(groups):
            for e in range(per):
                i = e * groups + p
                offset = pl.multiple_of(number_ref[1 + 2 * blocks + d * devices + i], SUB)
                slot = p * wide + e * win
                window[slot : slot + win, :] = recv_ref[i, pl.ds(offset, win), :]
        onehot = [
            jnp.where(spot == place_ref[d, p : p + 1, :] - d * rows, 1.0, 0.0).astype(jnp.bfloat16)
            for p in range(groups)
        ]
        onehot = jnp.concatenate(onehot, axis=1) if groups > 1 else onehot[0]
        placed = jnp.dot(onehot, window[...], preferred_element_type=jnp.float32)
        scaled = placed[:, :HD] * EXP2_SCALE
        high = scaled.astype(jnp.bfloat16)
        q_all[here, :HD] = high
        q_all[here, HD:] = (scaled - high.astype(jnp.float32)).astype(jnp.bfloat16)
        key = placed[:, HD : 2 * HD].astype(jnp.bfloat16)
        k_all[here, :HD] = key
        k_all[here, HD:] = key
        v_all[here, :HD] = placed[:, 2 * HD :].astype(jnp.bfloat16)

    def starting(index):
        return pl.multiple_of(index * block, block)

    def score(i, j, slot):
        scores[slot][...] = lax.dot_general(
            q_all[pl.ds(starting(i), block), :],
            k_all[pl.ds(starting(j), block), :],
            (((1,), (1,)), ((), ())),
            preferred_element_type=jnp.float32,
        )

    def mix(j, slot):
        mixed[...] = mixed[...] * fades[slot][...] + jnp.dot(
            weights[slot][...], v_all[pl.ds(starting(j), block), :HD], preferred_element_type=jnp.float32
        )

    def weigh(i, j, fresh, slot, diagonal, bounded):
        lane = lax.broadcasted_iota(jnp.int32, (part, HD), 1)
        down = lax.broadcasted_iota(jnp.int32, (part, HD), 0)
        for r in range(0, block, part):
            here = slice(r, r + part)
            if bounded:
                begin = begins[pl.ds(pl.multiple_of(i * block + r, part), part), :] - starting(j) - lane
            columns = []
            for n, cols in enumerate(lanes):
                if diagonal and n * HD >= r + part:
                    break
                raw = scores[slot][here, cols]
                if bounded:
                    raw = jnp.where(begin <= n * HD, raw, NEG)
                if diagonal and (n + 1) * HD > r + 1:
                    raw = jnp.where(lane - down <= r - n * HD, raw, NEG)
                columns.append(raw)
            peak = functools.reduce(jnp.maximum, columns)
            old = jnp.where(fresh, NEG, top[here, :])
            new = jnp.maximum(old, jnp.max(peak, axis=1, keepdims=True))
            fade = jnp.exp2(old - new)
            total = totals[1 - slot][here, :] * fade
            for n, cols in enumerate(lanes):
                if n < len(columns):
                    weight = jnp.exp2(columns[n] - new)
                    total += weight
                    weights[slot][here, cols] = weight.astype(jnp.bfloat16)
                else:
                    weights[slot][here, cols] = jnp.zeros((part, HD), jnp.bfloat16)
            top[here, :] = new
            fades[slot][here, :] = fade
            totals[slot][here, :] = total

    def finish(i, slot):
        total = jnp.sum(totals[slot][...], axis=1, keepdims=True)
        v_all[pl.ds(starting(i), block), HD:] = (mixed[...] / total).astype(jnp.bfloat16)

    def step(state, slot):
        last_i, last_j, i, j = state
        done = j == i
        next_i = jnp.where(done, jnp.minimum(i + 1, blocks - 1), i)
        next_j = jnp.where(done, low_of(next_i), j + 1)
        bounded = high_of(i) > j * block
        fresh = j == low_of(i)

        def work(diagonal, bounded):
            mix(last_j, 1 - slot)
            score(next_i, next_j, 1 - slot)
            weigh(i, j, fresh, slot, diagonal, bounded)

        @pl.when(done & bounded)
        def _():
            work(True, True)

        @pl.when(done & jnp.logical_not(bounded))
        def _():
            work(True, False)

        @pl.when(jnp.logical_not(done) & bounded)
        def _():
            work(False, True)

        @pl.when(jnp.logical_not(done | bounded))
        def _():
            work(False, False)

        @pl.when(last_j == last_i)
        def _():
            finish(last_i, 1 - slot)

        return i, j, next_i, next_j

    pairs = blocks * (blocks + 1) // 2
    for i in range(blocks):
        pairs -= low_of(i)
    mixed[...] = jnp.zeros_like(mixed)
    for slot in range(2):
        weights[slot][...] = jnp.zeros_like(weights[slot])
        fades[slot][...] = jnp.zeros_like(fades[slot])
        totals[slot][...] = jnp.zeros_like(totals[slot])
    top[...] = jnp.full_like(top, NEG)
    score(0, 0, 0)

    def two_steps(n, state):
        middle = step(state, 0)
        after = step_if(2 * n + 1 < pairs, middle)
        return after

    def step_if(more, state):
        _, _, i, j = state
        done = j == i
        next_i = jnp.where(done, jnp.minimum(i + 1, blocks - 1), i)
        next_j = jnp.where(done, low_of(next_i), j + 1)

        @pl.when(more)
        def _():
            step(state, 1)

        return i, j, next_i, next_j

    zero = jnp.int32(0)
    lax.fori_loop(0, (pairs + 1) // 2, two_steps, (zero + 1, zero, zero, zero))

    for slot in range(2):

        @pl.when(pairs % 2 == 1 - slot)
        def _():
            mix(blocks - 1, slot)
            finish(blocks - 1, slot)

    for k in range(span):
        owner = lax.rem(number_ref[0] + k, span)
        out_refs[k][...] = v_all[pl.ds(pl.multiple_of(owner * rows, SUB), rows), HD:]


def attend(received, after, numbers, places, first, rows, span, win, block):
    devices, total, _ = received.shape
    length = span * rows
    vmem = pl.BlockSpec(memory_space=pltpu.VMEM)
    smem = pl.BlockSpec(memory_space=pltpu.SMEM)
    narrow = pltpu.VMEM((block, HD), jnp.float32)
    return pl.pallas_call(
        functools.partial(attend_kernel, rows, span, win, block),
        out_shape=[jax.ShapeDtypeStruct((rows, HD), jnp.bfloat16)] * span,
        in_specs=[smem] + [vmem] * 3 + [pl.BlockSpec(memory_space=pl.ANY)] * len(after),
        out_specs=[vmem] * span,
        scratch_shapes=[
            pltpu.VMEM((length, 2 * HD), jnp.bfloat16),
            pltpu.VMEM((length, 2 * HD), jnp.bfloat16),
            pltpu.VMEM((length, 2 * HD), jnp.bfloat16),
            [pltpu.VMEM((devices * win, 3 * HD), jnp.bfloat16)] * 2,
            pltpu.VMEM((length, HD), jnp.int32),
            narrow,
            narrow,
            [pltpu.VMEM((block, block), jnp.float32)] * 2,
            [pltpu.VMEM((block, block), jnp.bfloat16)] * 2,
            [narrow] * 2,
            [narrow] * 2,
        ],
        compiler_params=pltpu.CompilerParams(vmem_limit_bytes=VMEM_LIMIT),
        cost_estimate=pl.CostEstimate(
            flops=2 * length * devices * win * 3 * HD + 8 * length * length * HD,
            bytes_accessed=2 * (devices * total * 3 * HD + length * HD),
            transcendentals=length * length // 2,
        ),
        name="attend_head",
    )(numbers, places, first.reshape(length // HD, HD), received, *after)


def join_kernel(span, own_ref, *refs):
    out_ref = refs[-1]
    for n, ref in enumerate(refs[:-1]):
        head = n // span * span + lax.rem(own_ref[0] + span - n % span, span)
        out_ref[:, pl.ds(pl.multiple_of(head * HD, HD), HD)] = ref[...]


def join_heads(own, pieces, span):
    vmem = pl.BlockSpec(memory_space=pltpu.VMEM)
    smem = pl.BlockSpec(memory_space=pltpu.SMEM)
    rows = pieces[0].shape[0]
    return pl.pallas_call(
        functools.partial(join_kernel, span),
        out_shape=jax.ShapeDtypeStruct((rows, len(pieces) * HD), jnp.bfloat16),
        in_specs=[smem] + [vmem] * len(pieces),
        out_specs=vmem,
        compiler_params=pltpu.CompilerParams(vmem_limit_bytes=VMEM_LIMIT),
        name="join_heads",
    )(own, *pieces)


def body(queries, keys, values, target_row, doc_lengths):
    rows, width = queries.shape
    group = width // HD
    devices = lax.axis_size("seq")
    span = max(group // 2, 1)
    units = devices // span
    each = group // span
    length = span * rows
    pair_most = 3 * rows // (2 * devices)
    mean = rows // units
    most = min(pair_most * span, rows)
    usual = min(mean + mean // 16, most)
    index = lax.axis_index("seq")
    own = (index % span).astype(jnp.int32).reshape(1)
    unit_start = index // span * length

    docs = jnp.arange(doc_lengths.shape[0])
    starts = jnp.sum(jnp.where(docs[:, None] < docs[None, :], doc_lengths[:, None], 0), axis=0)
    positions = unit_start + jnp.arange(length, dtype=jnp.int32)
    first = jnp.max(jnp.where(starts[None, :] <= positions[:, None], starts[None, :], 0), axis=1)
    first = jnp.maximum(first - unit_start, 0)
    block = math.gcd(length, 512)
    settings = jnp.concatenate([own, first[::block] // block, first[block - 1 :: block]])

    def homeward(piece, shift):
        if shift == 0:
            return piece
        route = [
            (u * span + m, u * span + (m + shift) % span) for u in range(units) for m in range(span)
        ]
        return lax.ppermute(piece, "seq", route)

    def attended(cap):
        total = rounded_up(cap + 3, SUB)
        win = SUB
        while win < pair_most + SUB - 1:
            win *= 2
        win = min(total, win)
        pieces = []
        after = []
        for chunk in range(each):
            sent = sort_rows(queries, keys, values, target_row, units, span, cap, total, chunk)
            received = lax.all_to_all(sent, "seq", split_axis=0, concat_axis=0, tiled=True)
            if chunk == 0:
                offsets, places, crowded = plan_rows(received, devices, span, rows, total, win)
                numbers = jnp.concatenate([settings, offsets])
            heads = attend(received, after, numbers, places, first, rows, span, win, block)
            after = [homeward(heads[shift], shift) for shift in range(span)]
            pieces += after
        return pieces, crowded

    pieces, crowded = attended(usual)
    if usual == most:
        return join_heads(own, pieces, span)
    return lax.cond(
        crowded,
        lambda: join_heads(own, attended(most)[0], span),
        lambda: join_heads(own, pieces, span),
    )


def solution(mesh):
    in_specs = (P("seq", "head"), P("seq", "head"), P("seq", "head"), P("seq"), P())
    out_specs = P("seq", "head")
    return jax.shard_map(body, mesh=mesh, in_specs=in_specs, out_specs=out_specs, check_vma=False)
```

```python
import functools
import math

import jax
import jax.numpy as jnp
from jax import lax
from jax.experimental import pallas as pl
from jax.experimental.pallas import tpu as pltpu
from jax.sharding import PartitionSpec as P

HD = 128
SUB = 16
BASE = 64
NEG = -1e30
EXP2_SCALE = math.log2(math.e) / math.sqrt(HD)
VMEM_LIMIT = 24 * 1024 * 1024
SORT_LIMIT = 60 * 1024 * 1024


def rounded_up(count, multiple):
    return -(-count // multiple) * multiple


def sort_kernel(units, span_rows, cap, total, target_ref, q_ref, k_ref, v_ref, out_ref, onehot, notes):
    rows = q_ref.shape[0]
    lanes = 3 * HD

    @pl.when(pl.program_id(0) == 0)
    def _():
        across = jnp.concatenate([target_ref[n : n + 1, :] for n in range(rows // HD)], axis=1)
        down = jnp.concatenate(
            [
                jnp.transpose(jnp.broadcast_to(target_ref[n : n + 1, :], (HD, HD)))
                for n in range(rows // HD)
            ],
            axis=0,
        )
        down = jnp.concatenate([down] * (rows // HD), axis=1)
        unit = jnp.zeros_like(across)
        for u in range(1, units):
            unit += (across >= u * span_rows).astype(jnp.int32)
        inner = across - unit * span_rows
        before = (down < across) & (down >= unit * span_rows)
        place = jnp.sum(before.astype(jnp.int32), axis=0, keepdims=True)
        slot = jnp.where(place < cap, unit * total + place, -1)
        slots = lax.broadcasted_iota(jnp.int32, (units * total, rows), 0)
        onehot[...] = jnp.where(slots == slot, 1.0, 0.0).astype(jnp.bfloat16)
        crowded = jnp.max(jnp.where(place >= cap, 1.0, 0.0), axis=1, keepdims=True)
        high = inner // BASE
        kind = lax.broadcasted_iota(jnp.int32, (SUB, rows), 0)
        digits = jnp.where(kind == 0, high + 1, jnp.where(kind == 1, inner - high * BASE, 0))
        digits = digits.astype(jnp.float32).astype(jnp.bfloat16)
        spread = lax.broadcasted_iota(jnp.int32, (lanes, rows), 0)
        line = lax.broadcasted_iota(jnp.int32, (total, lanes), 0)
        for u in range(units):
            mine = jnp.where((spread == place) & (unit == u), 1.0, 0.0).astype(jnp.bfloat16)
            along = lax.dot_general(
                digits, mine, (((1,), (1,)), ((), ())), preferred_element_type=jnp.float32
            )
            note = jnp.where(line == total - 3, along[0:1], jnp.where(line == total - 2, along[1:2], 0.0))
            note = jnp.where(line == total - 1, crowded, note)
            notes[u * total : (u + 1) * total, :] = note.astype(jnp.bfloat16)

    for m in range(q_ref.shape[1] // HD):
        cols = slice(m * HD, (m + 1) * HD)
        block = jnp.concatenate([q_ref[:, cols], k_ref[:, cols], v_ref[:, cols]], axis=1)
        sent = jnp.dot(onehot[...], block, preferred_element_type=jnp.float32).astype(jnp.bfloat16)
        out_ref[:, m] = (sent + notes[...]).reshape(units, total, lanes)


def sort_rows(queries, keys, values, target_row, units, span, cap, total, chunk):
    rows = queries.shape[0]
    steps = math.gcd(span, 2)
    count = span // steps
    column = pl.BlockSpec((rows, count * HD), lambda n: (0, chunk * steps + n))
    sent = pl.pallas_call(
        functools.partial(sort_kernel, units, span * rows, cap, total),
        grid=(steps,),
        out_shape=jax.ShapeDtypeStruct((units, span, total, 3 * HD), jnp.bfloat16),
        in_specs=[
            pl.BlockSpec((rows // HD, HD), lambda n: (0, 0)),
            column,
            column,
            column,
        ],
        out_specs=pl.BlockSpec((units, count, total, 3 * HD), lambda n: (0, n, 0, 0)),
        scratch_shapes=[
            pltpu.VMEM((units * total, rows), jnp.bfloat16),
            pltpu.VMEM((units * total, 3 * HD), jnp.bfloat16),
        ],
        compiler_params=pltpu.CompilerParams(vmem_limit_bytes=SORT_LIMIT),
        cost_estimate=pl.CostEstimate(
            flops=2 * units * span * total * rows * 3 * HD,
            bytes_accessed=2 * 3 * HD * span * (rows + units * total),
            transcendentals=0,
        ),
        name="sort_rows",
    )(target_row.reshape(rows // HD, HD), queries, keys, values)
    return sent.reshape(units * span, total, 3 * HD)


def plan_kernel(devices, span, rows, total, win, *refs):
    tail_ref, offset_ref, place_ref, crowded_ref = refs
    tail = tail_ref[...].astype(jnp.float32)
    lines = [tail[n, SUB - 3 :, :] for n in range(devices)]
    high = jnp.concatenate([line[0:1] for line in lines], axis=0)
    low = jnp.concatenate([line[1:2] for line in lines], axis=0)
    crowded = jnp.concatenate([line[2:3] for line in lines], axis=0)
    crowded_ref[...] = jnp.max(jnp.max(crowded, axis=1, keepdims=True), axis=0, keepdims=True).astype(jnp.int32)
    place = jnp.where(high > 0.0, (high - 1.0) * BASE + low, -1.0).astype(jnp.int32)
    per = max(HD // win, 1)
    groups = devices // per
    wide = per * win
    lane = lax.broadcasted_iota(jnp.int32, (groups, wide), 1)
    shifted = {}
    for t in range((total - win) // SUB + 1):
        for e in range(per):
            turn = (e * win - SUB * t) % (3 * HD)
            part = place[e * groups : (e + 1) * groups]
            shifted[t, e] = (pltpu.roll(part, turn, 1) if turn else part)[:, :wide]
    for d in range(span):
        begun = jnp.sum(jnp.where((place >= 0) & (place < d * rows), 1, 0), axis=1, keepdims=True)
        offset = jnp.minimum(begun // SUB * SUB, total - win)
        offset_ref[d] = jnp.broadcast_to(offset, (devices, HD))
        out = jnp.full((groups, wide), -1, jnp.int32)
        for (t, e), part in shifted.items():
            mine = (offset[e * groups : (e + 1) * groups] == SUB * t) & (lane >= e * win) & (lane < (e + 1) * win)
            out = jnp.where(mine, part, out)
        place_ref[d] = out


def plan_rows(received, devices, span, rows, total, win):
    wide = max(HD // win, 1) * win
    groups = devices * win // wide
    last = total // SUB - 1
    offsets, places, crowded = pl.pallas_call(
        functools.partial(plan_kernel, devices, span, rows, total, win),
        grid=(1,),
        out_shape=[
            jax.ShapeDtypeStruct((span, devices, HD), jnp.int32),
            jax.ShapeDtypeStruct((span, groups, wide), jnp.int32),
            jax.ShapeDtypeStruct((1, 1), jnp.int32),
        ],
        in_specs=[pl.BlockSpec((devices, SUB, 3 * HD), lambda n: (0, last, 0))],
        out_specs=[
            pl.BlockSpec((span, devices, HD), lambda n: (0, 0, 0)),
            pl.BlockSpec((span, groups, wide), lambda n: (0, 0, 0)),
            pl.BlockSpec((1, 1), lambda n: (0, 0)),
        ],
        compiler_params=pltpu.CompilerParams(vmem_limit_bytes=VMEM_LIMIT),
        name="plan_rows",
    )(received)
    return offsets[:, :, 0].reshape(-1), places, crowded[0, 0] > 0


def attend_kernel(rows, span, win, block, number_ref, place_ref, first_ref, recv_ref, *refs):
    out_refs = refs[-11 - span : -11]
    q_all, k_all, v_all, windows, begins, top, mixed, scores, weights, fades, totals = refs[-11:]
    devices = recv_ref.shape[0]
    groups, wide = place_ref.shape[1:]
    per = wide // win
    blocks = span * rows // block
    lanes = [slice(n * HD, (n + 1) * HD) for n in range(block // HD)]

    def low_of(i):
        return number_ref[1 + i]

    def high_of(i):
        return number_ref[1 + blocks + i]

    part = min(64, block)

    @pl.when(high_of(blocks - 1) > 0)
    def _():
        for n in range(span * rows // HD):
            begin = jnp.broadcast_to(first_ref[n : n + 1, :], (HD, HD))
            begins[n * HD : (n + 1) * HD, :] = jnp.transpose(begin)

    spot = lax.broadcasted_iota(jnp.int32, (rows, wide), 0)
    for d in range(span):
        here = slice(d * rows, (d + 1) * rows)
        window = windows[d % 2]
        for p in range(groups):
            for e in range(per):
                i = e * groups + p
                offset = pl.multiple_of(number_ref[1 + 2 * blocks + d * devices + i], SUB)
                slot = p * wide + e * win
                window[slot : slot + win, :] = recv_ref[i, pl.ds(offset, win), :]
        onehot = [
            jnp.where(spot == place_ref[d, p : p + 1, :] - d * rows, 1.0, 0.0).astype(jnp.bfloat16)
            for p in range(groups)
        ]
        onehot = jnp.concatenate(onehot, axis=1) if groups > 1 else onehot[0]
        placed = jnp.dot(onehot, window[...], preferred_element_type=jnp.float32)
        scaled = placed[:, :HD] * EXP2_SCALE
        high = scaled.astype(jnp.bfloat16)
        q_all[here, :HD] = high
        q_all[here, HD:] = (scaled - high.astype(jnp.float32)).astype(jnp.bfloat16)
        key = placed[:, HD : 2 * HD].astype(jnp.bfloat16)
        k_all[here, :HD] = key
        k_all[here, HD:] = key
        v_all[here, :HD] = placed[:, 2 * HD :].astype(jnp.bfloat16)

    def starting(index):
        return pl.multiple_of(index * block, block)

    def score(i, j, slot):
        scores[slot][...] = lax.dot_general(
            q_all[pl.ds(starting(i), block), :],
            k_all[pl.ds(starting(j), block), :],
            (((1,), (1,)), ((), ())),
            preferred_element_type=jnp.float32,
        )

    def mix(j, slot):
        mixed[...] = mixed[...] * fades[slot][...] + jnp.dot(
            weights[slot][...], v_all[pl.ds(starting(j), block), :HD], preferred_element_type=jnp.float32
        )

    def weigh(i, j, fresh, slot, diagonal, bounded):
        lane = lax.broadcasted_iota(jnp.int32, (part, HD), 1)
        down = lax.broadcasted_iota(jnp.int32, (part, HD), 0)
        for r in range(0, block, part):
            here = slice(r, r + part)
            if bounded:
                begin = begins[pl.ds(pl.multiple_of(i * block + r, part), part), :] - starting(j) - lane
            columns = []
            for n, cols in enumerate(lanes):
                if diagonal and n * HD >= r + part:
                    break
                raw = scores[slot][here, cols]
                if bounded:
                    raw = jnp.where(begin <= n * HD, raw, NEG)
                if diagonal and (n + 1) * HD > r + 1:
                    raw = jnp.where(lane - down <= r - n * HD, raw, NEG)
                columns.append(raw)
            peak = functools.reduce(jnp.maximum, columns)
            old = jnp.where(fresh, NEG, top[here, :])
            new = jnp.maximum(old, jnp.max(peak, axis=1, keepdims=True))
            fade = jnp.exp2(old - new)
            total = totals[1 - slot][here, :] * fade
            for n, cols in enumerate(lanes):
                if n < len(columns):
                    weight = jnp.exp2(columns[n] - new)
                    total += weight
                    weights[slot][here, cols] = weight.astype(jnp.bfloat16)
                else:
                    weights[slot][here, cols] = jnp.zeros((part, HD), jnp.bfloat16)
            top[here, :] = new
            fades[slot][here, :] = fade
            totals[slot][here, :] = total

    def finish(i, slot):
        total = jnp.sum(totals[slot][...], axis=1, keepdims=True)
        v_all[pl.ds(starting(i), block), HD:] = (mixed[...] / total).astype(jnp.bfloat16)

    def step(state, slot):
        last_i, last_j, i, j = state
        done = j == i
        next_i = jnp.where(done, jnp.minimum(i + 1, blocks - 1), i)
        next_j = jnp.where(done, low_of(next_i), j + 1)
        bounded = high_of(i) > j * block
        fresh = j == low_of(i)

        def work(diagonal, bounded):
            mix(last_j, 1 - slot)
            score(next_i, next_j, 1 - slot)
            weigh(i, j, fresh, slot, diagonal, bounded)

        @pl.when(done & bounded)
        def _():
            work(True, True)

        @pl.when(done & jnp.logical_not(bounded))
        def _():
            work(True, False)

        @pl.when(jnp.logical_not(done) & bounded)
        def _():
            work(False, True)

        @pl.when(jnp.logical_not(done | bounded))
        def _():
            work(False, False)

        @pl.when(last_j == last_i)
        def _():
            finish(last_i, 1 - slot)

        return i, j, next_i, next_j

    pairs = blocks * (blocks + 1) // 2
    for i in range(blocks):
        pairs -= low_of(i)
    mixed[...] = jnp.zeros_like(mixed)
    for slot in range(2):
        weights[slot][...] = jnp.zeros_like(weights[slot])
        fades[slot][...] = jnp.zeros_like(fades[slot])
        totals[slot][...] = jnp.zeros_like(totals[slot])
    top[...] = jnp.full_like(top, NEG)
    score(0, 0, 0)

    def two_steps(n, state):
        middle = step(state, 0)
        after = step_if(2 * n + 1 < pairs, middle)
        return after

    def step_if(more, state):
        _, _, i, j = state
        done = j == i
        next_i = jnp.where(done, jnp.minimum(i + 1, blocks - 1), i)
        next_j = jnp.where(done, low_of(next_i), j + 1)

        @pl.when(more)
        def _():
            step(state, 1)

        return i, j, next_i, next_j

    zero = jnp.int32(0)
    lax.fori_loop(0, (pairs + 1) // 2, two_steps, (zero + 1, zero, zero, zero))

    for slot in range(2):

        @pl.when(pairs % 2 == 1 - slot)
        def _():
            mix(blocks - 1, slot)
            finish(blocks - 1, slot)

    for k in range(span):
        owner = lax.rem(number_ref[0] + k, span)
        out_refs[k][...] = v_all[pl.ds(pl.multiple_of(owner * rows, SUB), rows), HD:]


def attend(received, after, numbers, places, first, rows, span, win, block):
    devices, total, _ = received.shape
    length = span * rows
    vmem = pl.BlockSpec(memory_space=pltpu.VMEM)
    smem = pl.BlockSpec(memory_space=pltpu.SMEM)
    narrow = pltpu.VMEM((block, HD), jnp.float32)
    return pl.pallas_call(
        functools.partial(attend_kernel, rows, span, win, block),
        out_shape=[jax.ShapeDtypeStruct((rows, HD), jnp.bfloat16)] * span,
        in_specs=[smem] + [vmem] * 3 + [pl.BlockSpec(memory_space=pl.ANY)] * len(after),
        out_specs=[vmem] * span,
        scratch_shapes=[
            pltpu.VMEM((length, 2 * HD), jnp.bfloat16),
            pltpu.VMEM((length, 2 * HD), jnp.bfloat16),
            pltpu.VMEM((length, 2 * HD), jnp.bfloat16),
            [pltpu.VMEM((devices * win, 3 * HD), jnp.bfloat16)] * 2,
            pltpu.VMEM((length, HD), jnp.int32),
            narrow,
            narrow,
            [pltpu.VMEM((block, block), jnp.float32)] * 2,
            [pltpu.VMEM((block, block), jnp.bfloat16)] * 2,
            [narrow] * 2,
            [narrow] * 2,
        ],
        compiler_params=pltpu.CompilerParams(vmem_limit_bytes=VMEM_LIMIT),
        cost_estimate=pl.CostEstimate(
            flops=2 * length * devices * win * 3 * HD + 8 * length * length * HD,
            bytes_accessed=2 * (devices * total * 3 * HD + length * HD),
            transcendentals=length * length // 2,
        ),
        name="attend_head",
    )(numbers, places, first.reshape(length // HD, HD), received, *after)


def join_kernel(span, own_ref, *refs):
    out_ref = refs[-1]
    for n, ref in enumerate(refs[:-1]):
        head = n // span * span + lax.rem(own_ref[0] + span - n % span, span)
        out_ref[:, pl.ds(pl.multiple_of(head * HD, HD), HD)] = ref[...]


def join_heads(own, pieces, span):
    vmem = pl.BlockSpec(memory_space=pltpu.VMEM)
    smem = pl.BlockSpec(memory_space=pltpu.SMEM)
    rows = pieces[0].shape[0]
    return pl.pallas_call(
        functools.partial(join_kernel, span),
        out_shape=jax.ShapeDtypeStruct((rows, len(pieces) * HD), jnp.bfloat16),
        in_specs=[smem] + [vmem] * len(pieces),
        out_specs=vmem,
        compiler_params=pltpu.CompilerParams(vmem_limit_bytes=VMEM_LIMIT),
        name="join_heads",
    )(own, *pieces)


def body(queries, keys, values, target_row, doc_lengths):
    rows, width = queries.shape
    group = width // HD
    devices = lax.axis_size("seq")
    span = max(group // 2, 1)
    units = devices // span
    each = group // span
    length = span * rows
    pair_most = 3 * rows // (2 * devices)
    mean = rows // units
    most = min(pair_most * span, rows)
    usual = min(mean + mean // 16, most)
    index = lax.axis_index("seq")
    own = (index % span).astype(jnp.int32).reshape(1)
    unit_start = index // span * length

    docs = jnp.arange(doc_lengths.shape[0])
    starts = jnp.sum(jnp.where(docs[:, None] < docs[None, :], doc_lengths[:, None], 0), axis=0)
    positions = unit_start + jnp.arange(length, dtype=jnp.int32)
    first = jnp.max(jnp.where(starts[None, :] <= positions[:, None], starts[None, :], 0), axis=1)
    first = jnp.maximum(first - unit_start, 0)
    block = math.gcd(length, 512)
    settings = jnp.concatenate([own, first[::block] // block, first[block - 1 :: block]])

    def homeward(piece, shift):
        if shift == 0:
            return piece
        route = [
            (u * span + m, u * span + (m + shift) % span) for u in range(units) for m in range(span)
        ]
        return lax.ppermute(piece, "seq", route)

    def attended(cap):
        total = rounded_up(cap + 3, SUB)
        win = SUB
        while win < pair_most + SUB - 1:
            win *= 2
        win = min(total, win)
        pieces = []
        after = []
        for chunk in range(each):
            sent = sort_rows(queries, keys, values, target_row, units, span, cap, total, chunk)
            received = lax.all_to_all(sent, "seq", split_axis=0, concat_axis=0, tiled=True)
            if chunk == 0:
                offsets, places, crowded = plan_rows(received, devices, span, rows, total, win)
                numbers = jnp.concatenate([settings, offsets])
            heads = attend(received, after, numbers, places, first, rows, span, win, block)
            after = [homeward(heads[shift], shift) for shift in range(span)]
            pieces += after
        return pieces, crowded

    pieces, crowded = attended(usual)
    if usual == most:
        return join_heads(own, pieces, span)
    return lax.cond(
        crowded,
        lambda: join_heads(own, attended(most)[0], span),
        lambda: join_heads(own, pieces, span),
    )


def solution(mesh):
    in_specs = (P("seq", "head"), P("seq", "head"), P("seq", "head"), P("seq"), P())
    out_specs = P("seq", "head")
    return jax.shard_map(body, mesh=mesh, in_specs=in_specs, out_specs=out_specs, check_vma=False)
```
